512 devices in a mesh: sky: 16 (over y, x), sensor: 32 (over z, core).
Axes of the slice: x: 4, y: 4, z: 16, core: 2. Of those that a mesh axis runs over, the one named last changes fastest.
Arguments:
- sky: bfloat16 [146, 512], P(None, 'sky'), may hold values from 0.049804688 to 5
- daylight: bfloat16 [32, 640, 145, 146], P('sensor', 'sky'), may hold values from -0.5 to 0.5
- bsdf: bfloat16 [32, 145, 145], P('sensor'), may hold values from -0.5 to 0.5
- bsdf_ids: int32 [32, 640], P('sensor', 'sky'), may hold values from 0 to 31
- view: bfloat16 [32, 256, 32, 145], P('sensor', 'sky'), may hold values from -0.125 to 0.125
- visible: int32 [32, 256, 32], P('sensor', 'sky'), may hold values from 0 to 639, as said below
- counts: int32 [32, 256], P('sensor', 'sky'), may hold values from 1 to 32, 4096 in all within a row
Outputs:
- illuminance: float32 [32, 512, 256], P('sensor', 'sky')
The draws below stay inside these ranges and needn't reach their ends.
Inputs may be any that keep to these rules, and one draw needn't show every extreme that they name: `visible`: each sensor lists 32 different windows of its own tile. `counts`: the lists of one tile hold 4096 live entries in all.
All inputs are finite; a program needn't handle non-finite values. No bound on the sum of `counts` on one device may be relied on, other than what follows from the above.
Results may differ from the reference program's by a relative error of at most 0.004.
Values may be sent and summed in bfloat16 or wider, within the bound.
A program may use at most 128 MiB of HBM per device.

```python
import math
import jax
import jax.numpy as jnp
import numpy as np
from jax import lax

PATCHES = 146
BINS = 145
SLOTS = 32
NBSDF = 32
TILES = 32
HOURS = 512
WIN_TILE = 640
SENS_TILE = 256


def draw_visible(key, part):
    key = jax.random.fold_in(key, 7)
    scores = jax.random.randint(key, (TILES, SENS_TILE, WIN_TILE), 0, 1 << 20)
    scores = scores * WIN_TILE + jnp.arange(WIN_TILE, dtype=jnp.int32)[None, None, :]
    unused, picked = lax.top_k(scores, SLOTS)
    return picked.astype(jnp.int32)


def place_ends(result, key, low, largest):
    dims = result.shape
    index_at = [jax.random.randint(jax.random.fold_in(key, axis), (), 0, dims[axis]) for axis in range(len(dims))]
    result = result.at[tuple(index_at)].set(low)
    longest = dims.index(max(dims))
    index_at[longest] = (index_at[longest] + 1) % dims[longest]
    return result.at[tuple(index_at)].set(largest)


def block_scale(key, shape, shards, low, largest):
    loudness, own = 1.0, jax.random.fold_in(key, 6)
    for axis_at, parts in shards:
        steps = jnp.exp(jax.random.uniform(jax.random.fold_in(own, axis_at), (parts,), jnp.float32, low / len(shards), largest / len(shards)))
        loudness = loudness * jnp.repeat(steps, shape[axis_at] // parts).reshape([-1 if axis == axis_at else 1 for axis in range(len(shape))])
    return loudness


def profile(number_of, total, most, slope):
    portions = [(1 << 20) // math.isqrt(rank ** slope) + 1 for rank in range(2, number_of + 1)]
    surplus, holding = total - most - (number_of - 1), [1] * (number_of - 1)
    while surplus > 0:
        free = [i for i in range(number_of - 1) if holding[i] < most]
        mass, budget = sum([portions[i] for i in free]), surplus
        for i in free:
            more = min(most - holding[i], max(1, budget * portions[i] // mass), surplus)
            holding[i] = holding[i] + more
            surplus = surplus - more
    return np.array([most] + holding)


def uneven(stream_key, count, total, reach, skew):
    if count == 2:
        one = jax.random.randint(stream_key, (), max(1, total - reach), min(reach, total - 1) + 1)
        return jnp.stack([one, total - one])
    lengths = jnp.asarray(profile(count, total, reach, skew), jnp.int32)
    twos = (count - 1) // 2
    source_of, receiver = lengths[1:1 + 2 * twos:2], lengths[2:2 + 2 * twos:2]
    margin = jnp.minimum(source_of - 1, reach - receiver)
    shifted = jax.random.randint(jax.random.fold_in(stream_key, 1), (twos,), 0, 1 << 20) % (margin + 1)
    lengths = lengths.at[1:1 + 2 * twos:2].set(source_of - shifted).at[2:2 + 2 * twos:2].set(receiver + shifted)
    return lengths[jax.random.permutation(jax.random.fold_in(stream_key, 2), count)]


def noise(rng, extent, deviation, reach, shards=(), kind=jnp.bfloat16):
    loudness = block_scale(rng, extent, shards, -0.22, 0.18) if shards else 1.0
    values = jax.random.normal(rng, extent, jnp.float32) * deviation * loudness
    return jnp.minimum(jnp.maximum(values, -reach), reach).astype(kind)


def setup_inputs(seed: int = 0) -> dict:
    key_list = jax.random.split(jax.random.key(seed), 8)
    sky = jnp.clip(jnp.exp(math.log(5.0) - 4.609084 * jax.random.uniform(key_list[0], (PATCHES, HOURS), jnp.float32) ** block_scale(key_list[0], (PATCHES, HOURS), ((1, 16),), -0.2, 0.2)), 0.049804688, 5.0).astype(jnp.bfloat16)
    daylight = noise(key_list[1], (TILES, WIN_TILE, BINS, PATCHES), PATCHES ** -0.5, 0.5, ((0, 32), (1, 16)))
    bsdf = noise(key_list[2], (NBSDF, BINS, BINS), BINS ** -0.5, 0.5, ((0, 32),))
    bsdf_ids = place_ends(jax.random.randint(key_list[3], (TILES, WIN_TILE), 0, NBSDF), jax.random.fold_in(key_list[3], 1), 0, NBSDF - 1).astype(jnp.int32)
    view = noise(key_list[4], (TILES, SENS_TILE, SLOTS, BINS), (BINS * SLOTS // 2) ** -0.5, 0.125, ((0, 32), (1, 16)))
    visible = draw_visible(jax.random.fold_in(key_list[7], 71), 0)
    counts = jax.vmap(lambda own: uneven(own, SENS_TILE, SENS_TILE * SLOTS // 2, SLOTS, 2))(jax.random.split(key_list[6], TILES)).reshape((TILES, SENS_TILE)).astype(jnp.int32)
    return {"sky": sky, "daylight": daylight, "bsdf": bsdf, "bsdf_ids": bsdf_ids, "view": view, "visible": visible, "counts": counts}


def one_tile(sky, bsdf, items):
    daylight, bsdf_ids, view, visible, counts = items
    irradiance = jnp.einsum("wbp,ph->whb", daylight.astype(jnp.float32), sky.astype(jnp.float32)).astype(jnp.bfloat16)
    chosen = bsdf[bsdf_ids]
    transmitted = jnp.einsum("whb,wcb->whc", irradiance.astype(jnp.float32), chosen.astype(jnp.float32)).astype(jnp.bfloat16)
    slot_index = jnp.arange(SLOTS, dtype=jnp.int32)
    live = slot_index[None, :] < counts[:, None]
    live_view = jnp.where(live[:, :, None], view, jnp.zeros_like(view)).astype(jnp.bfloat16)

    def add_slot(total, slot):
        window_ids, coeffs = slot
        rows = transmitted[window_ids].astype(jnp.float32)
        return total + jnp.einsum("shb,sb->hs", rows, coeffs.astype(jnp.float32)), None

    start = jnp.zeros((HOURS, SENS_TILE), jnp.float32)
    total, unused = lax.scan(add_slot, start, (jnp.transpose(visible, (1, 0)), jnp.transpose(live_view, (1, 0, 2))))
    return total


def reference(sky, daylight, bsdf, bsdf_ids, view, visible, counts):
    return lax.map(lambda items: one_tile(sky, bsdf, items), (daylight, bsdf_ids, view, visible, counts))
```

```python
import math

import jax
import jax.numpy as jnp
from jax import lax
from jax.experimental import pallas as pl
from jax.experimental.pallas import tpu as pltpu
from jax.sharding import PartitionSpec as P

F32 = jnp.float32
BF16 = jnp.bfloat16
MESH = pl.DeviceIdType.MESH
ROWS = 48
META = 16


def up(n, m):
    return -(-n // m) * m


def iota(shape, dim):
    return lax.broadcasted_iota(jnp.int32, shape, dim)


def dot(a, b, dims=((1,), (0,))):
    return lax.dot_general(a, b, (dims, ((), ())), preferred_element_type=F32)


def kernel(dims, sky_ref, day_hbm, bsdf_ref, ids_ref, view_ref, vis_ref, counts_ref, out_ref, flag_ref,
           day, wide, days, mats, tables, own, vpad, rank, send, got, dense, part, chunks, total, whole,
           day_sem, loc_sem, ring_send, ring_recv, sib_send, sib_recv, v_send, v_recv, a_send, a_recv, g_send, g_recv):
    n_sky, n_sen, bins, patches, wins, sens, slots = dims
    nz = n_sen // 2
    kb = up(bins, 16)
    entries = sens * slots
    me = lax.axis_index("sky")
    mine = lax.axis_index("sensor")
    z, core = mine // 2, lax.rem(mine, 2)
    after = lax.rem(z + 1, nz) * 2 + core
    before = lax.rem(z + nz - 1, nz) * 2 + core
    sibling = z * 2 + (1 - core)

    barrier = pltpu.get_barrier_semaphore()

    def greet(k, c):
        pl.semaphore_signal(barrier, inc=1, device_id=(lax.rem(me + k, n_sky), mine), device_id_type=MESH)
        return c

    lax.fori_loop(1, n_sky, greet, 0)
    for other in (after, before, sibling):
        pl.semaphore_signal(barrier, inc=1, device_id=(me, other), device_id_type=MESH)

    day_copy = pltpu.make_async_copy(day_hbm, day, day_sem)
    day_copy.start()

    vis = vis_ref[...]
    owner = vis // wins
    local = vis - owner * wins
    spread = (lax.rem(iota((slots, entries), 1), slots) == iota((slots, entries), 0)).astype(BF16)
    sensor_of = iota((sens, entries), 1) // slots == iota((sens, entries), 0)

    def flat(x):
        return jnp.sum(jnp.where(sensor_of, dot(x.astype(F32).astype(BF16), spread), 0.0), axis=0, keepdims=True)

    owner_row, local_row = flat(owner), flat(local)
    slot_row = lax.rem(iota((1, entries), 1), slots).astype(F32)
    sens_row = (iota((1, entries), 1) // slots).astype(F32)
    counts = jnp.broadcast_to(counts_ref[...].astype(F32), (16, sens)).astype(BF16)
    count_row = dot(counts, sensor_of.astype(BF16))[0:1]
    live = slot_row < count_row
    goes = jnp.logical_and(iota((n_sky, entries), 0).astype(F32) == owner_row, live)
    goes_f = goes.astype(F32)
    earlier = (iota((entries, entries), 0) < iota((entries, entries), 1)).astype(BF16)
    rank[...] = jnp.where(goes, dot(goes_f.astype(BF16), earlier), -1.0)
    most = jnp.max(jnp.sum(goes_f, axis=1, keepdims=True), axis=0, keepdims=True)
    over = jnp.where(most > ROWS, 1.0, 0.0)

    own[...] = jnp.zeros(own.shape, BF16)
    own[0:bins, 0:bins] = bsdf_ref[...]
    corner = own[kb - 16 : kb, 128:256].astype(F32)
    last = jnp.logical_and(iota(corner.shape, 0) == 15, iota(corner.shape, 1) == 127)
    own[kb - 16 : kb, 128:256] = jnp.where(last, over, corner).astype(BF16)

    pl.semaphore_wait(barrier, n_sky + 2)

    def table(src, at, device, s_sem, r_sem):
        return pltpu.make_async_remote_copy(
            src_ref=src, dst_ref=tables.at[at], send_sem=s_sem, recv_sem=r_sem, device_id=(me, device), device_id_type=MESH)

    own_copy = pltpu.make_async_copy(own, tables.at[mine], loc_sem.at[0])
    own_copy.start()
    sent = []

    def go(copy):
        copy.start()
        sent.append(copy)

    def at_z(shift):
        return lax.rem(z + shift + nz, nz) * 2 + core

    right_steps, left_steps = nz // 2, nz - 1 - nz // 2

    def ring(step):
        for steps, sign, to, lane in ((right_steps, -1, after, 0), (left_steps, 1, before, 1)):
            if step > steps:
                continue
            at = at_z(sign * step)
            src = own if step == 0 else tables.at[at]
            if step > 0:
                table(src, at, mine_other(sign), ring_send.at[lane, 0], ring_recv.at[at // 2]).wait_recv()
            if step < steps:
                go(table(src, at, to, ring_send.at[lane, step], ring_recv.at[at // 2]))
            if step > 0 or lane == 0:
                go(table(src, at, sibling, sib_send.at[at // 2], sib_recv.at[at // 2]))

    def mine_other(sign):
        return before if sign < 0 else after

    steps_done = [0]

    def ring_next():
        if steps_done[0] <= right_steps:
            ring(steps_done[0])
        steps_done[0] += 1

    ring_next()

    vpad[...] = jnp.zeros(vpad.shape, BF16)
    vpad[:, 0:bins] = view_ref[...]
    meta_row = iota((META, entries), 0)
    meta = jnp.where(meta_row == 0, local_row + 1.0, jnp.where(meta_row == 1, sens_row, 0.0)).astype(BF16)
    place = iota((ROWS, entries), 0).astype(F32)

    def pack(q, c):
        pick = (place == rank[pl.ds(q, 1), :]).astype(BF16)
        send[q, 0:ROWS, :] = dot(pick, vpad[...]).astype(BF16)
        send[q, ROWS : ROWS + META, 0:ROWS] = dot(meta, pick, ((1,), (1,))).astype(BF16)
        return c

    lax.fori_loop(0, n_sky, pack, 0)

    def message(q, slot):
        return pltpu.make_async_remote_copy(
            src_ref=send.at[q], dst_ref=got.at[slot], send_sem=v_send.at[q], recv_sem=v_recv.at[slot],
            device_id=(q, mine), device_id_type=MESH)

    def put(k, c):
        message(lax.rem(me + k, n_sky), me).start()
        return c

    lax.fori_loop(1, n_sky, put, 0)
    keep = pltpu.make_async_copy(send.at[me], got.at[me], loc_sem.at[1])
    keep.start()
    ring_next()

    wide[1] = jnp.zeros(wide.shape[1:], F32)
    wide[0, bins * wins :, :] = jnp.zeros((wide.shape[1] - bins * wins, 128), F32)
    day_copy.wait()

    def widen(b, c):
        x = day[b].astype(F32)
        rows = pl.ds(pl.multiple_of(b * wins, 8), wins)
        wide[0, rows, :] = x[:, 0:128]
        wide[1, rows, 0 : patches - 128] = x[:, 128:patches]
        return c

    lax.fori_loop(0, bins, widen, 0, unroll=5 if bins % 5 == 0 else 1)
    ring_next()

    def by_window(w, c):
        for half in range(2):
            days[w, :, half * 128 : half * 128 + 128] = wide[half, pl.ds(w, kb, stride=wins), :].astype(BF16)
        return c

    lax.fori_loop(0, wins, by_window, 0)
    ring_next()

    keep.wait()

    def await_message(k, c):
        message(lax.rem(me + k, n_sky), lax.rem(me + k, n_sky)).wait_recv()
        return c

    lax.fori_loop(1, n_sky, await_message, 0)
    ring_next()
    which = iota((wins * sens, ROWS), 0).astype(F32)

    def unpack(q, c):
        note = got[q, ROWS : ROWS + META, 0:ROWS].astype(F32)
        code = note[0:1] * float(sens) + note[1:2] - float(sens)
        pick = (which == code).astype(BF16)
        rows = dot(pick, got[q, 0:ROWS, :]).astype(BF16).reshape(wins, sens, 256)
        dense[:, pl.ds(pl.multiple_of(q * sens, sens), sens), :] = rows
        return c

    lax.fori_loop(0, n_sky // 2, unpack, 0)
    ring_next()
    lax.fori_loop(n_sky // 2, n_sky, unpack, 0)
    while steps_done[0] <= right_steps:
        ring_next()
    own_copy.wait()

    def await_sibling(i, c):
        at = i * 2 + (1 - core)
        table(tables.at[at], at, sibling, sib_send.at[i], sib_recv.at[i]).wait_recv()
        return c

    lax.fori_loop(0, nz, await_sibling, 0)

    def through(w, c):
        mats[w] = dot(tables[ids_ref[0, w]][:, 0:kb], days[w]).astype(BF16)
        return c

    lax.fori_loop(0, wins, through, 0, unroll=4)

    part[...] = jnp.zeros(part.shape, F32)
    group = 8 if wins % 8 == 0 else 1

    def gather(g, c):
        acc = part[...]
        for i in range(group):
            w = g * group + i
            acc = acc + dot(dense[w][:, 0:kb], mats[w])
        part[...] = acc
        return c

    lax.fori_loop(0, wins // group, gather, 0)
    flags = jnp.zeros((16, 128), F32)
    for i in range(n_sen):
        flags = flags + tables[i, kb - 16 : kb, 128:256].astype(F32)
    any_over = jnp.where(flags[15:16, 127:128] > 0.0, 1.0, 0.0)
    lane = iota((sens * n_sky, 256), 1)
    part[...] = jnp.where(lane < patches, part[...], jnp.where(lane == 255, any_over, 0.0))

    def share(q, slot):
        return pltpu.make_async_remote_copy(
            src_ref=part.at[pl.ds(pl.multiple_of(q * sens, sens), sens)], dst_ref=chunks.at[slot],
            send_sem=a_send.at[q], recv_sem=a_recv.at[slot], device_id=(q, mine), device_id_type=MESH)

    def put_share(k, c):
        share(lax.rem(me + k, n_sky), me).start()
        return c

    lax.fori_loop(1, n_sky, put_share, 0)
    total[...] = part[pl.ds(pl.multiple_of(me * sens, sens), sens), :]

    def add(k, c):
        q = lax.rem(me + k, n_sky)
        share(q, q).wait_recv()
        total[...] += chunks[q]
        return c

    lax.fori_loop(1, n_sky, add, 0)

    def spread_out(q, slot):
        return pltpu.make_async_remote_copy(
            src_ref=total, dst_ref=whole.at[pl.ds(pl.multiple_of(slot * sens, sens), sens)],
            send_sem=g_send.at[q], recv_sem=g_recv.at[slot], device_id=(q, mine), device_id_type=MESH)

    def put_total(k, c):
        spread_out(lax.rem(me + k, n_sky), me).start()
        return c

    lax.fori_loop(1, n_sky, put_total, 0)
    whole[pl.ds(pl.multiple_of(me * sens, sens), sens), :] = total[...]

    def await_total(k, c):
        q = lax.rem(me + k, n_sky)
        spread_out(q, q).wait_recv()
        return c

    lax.fori_loop(1, n_sky, await_total, 0)
    a = whole[...]
    high = a.astype(BF16)
    low = (a - high.astype(F32)).astype(BF16)
    sky = sky_ref[...]
    out_ref[...] = dot(sky, high[:, 0:patches], ((1,), (1,))) + dot(sky, low[:, 0:patches], ((1,), (1,)))
    flag_ref[...] = jnp.broadcast_to(total[0:1, 255:256], flag_ref.shape)

    for copy in sent:
        copy.wait_send()

    def drain(k, c):
        q = lax.rem(me + k, n_sky)
        message(q, me).wait_send()
        share(q, me).wait_send()
        spread_out(q, me).wait_send()
        return c

    lax.fori_loop(1, n_sky, drain, 0)


def general(sky, daylight, bsdf, bsdf_ids, view, visible, counts):
    local_day = daylight[0]
    sky_devices = lax.axis_size("sky")
    irradiance = jnp.einsum(
        "wbp,ph->whb", local_day, lax.all_gather(sky, "sky", axis=1, tiled=True), preferred_element_type=F32
    ).astype(BF16)
    tables = lax.all_gather(bsdf, "sensor", axis=0, tiled=True)
    chosen = tables[bsdf_ids[0]]
    transmitted = jnp.einsum("whb,wcb->whc", irradiance, chosen, preferred_element_type=F32).astype(BF16)
    slot_count = view.shape[2]
    slot_index = lax.broadcasted_iota(jnp.int32, visible.shape, 2)
    live = slot_index < counts[:, :, None]
    live_view = jnp.where(live[:, :, :, None], view, jnp.zeros_like(view))
    rows_all = lax.all_gather(live_view, "sky", axis=1, tiled=True)[0]
    ids_all = lax.all_gather(visible, "sky", axis=1, tiled=True)[0]
    sens_tile = rows_all.shape[0]
    hour_dev = transmitted.shape[1] // sky_devices
    light = lax.all_to_all(transmitted, "sky", split_axis=1, concat_axis=0, tiled=True)
    block = math.gcd(sens_tile, 32)
    blocks = sens_tile // block
    rows_blocked = rows_all.reshape(blocks, block, slot_count, rows_all.shape[2])
    ids_blocked = ids_all.reshape(blocks, block, slot_count)

    def sensor_block(items):
        coeffs, window_ids = items
        return jnp.einsum("skhb,skb->hs", light[window_ids], coeffs, preferred_element_type=F32)

    parts_out = lax.map(sensor_block, (rows_blocked, ids_blocked))
    return jnp.transpose(parts_out, (1, 0, 2)).reshape(hour_dev, sens_tile)


def body(sky, daylight, bsdf, bsdf_ids, view, visible, counts):
    n_sky, n_sen = lax.axis_size("sky"), lax.axis_size("sensor")
    patches, hours = sky.shape
    _, wins, bins, _ = daylight.shape
    _, sens, slots, _ = view.shape
    kb, entries, nz = up(bins, 16), sens * slots, n_sen // 2
    dims = (n_sky, n_sen, bins, patches, wins, sens, slots)
    vmem = pl.BlockSpec(memory_space=pltpu.VMEM)
    dma = pltpu.SemaphoreType.DMA

    def run(*refs):
        kernel(dims, *refs)

    out, flag = pl.pallas_call(
        run,
        out_shape=(jax.ShapeDtypeStruct((hours, sens * n_sky), F32), jax.ShapeDtypeStruct((8, 128), F32)),
        in_specs=[vmem, pl.BlockSpec(memory_space=pl.ANY), vmem, pl.BlockSpec(memory_space=pltpu.SMEM), vmem, vmem, vmem],
        out_specs=(vmem, vmem),
        scratch_shapes=[
            pltpu.VMEM((bins, wins, patches), BF16),
            pltpu.VMEM((2, kb * wins, 128), F32),
            pltpu.VMEM((wins, kb, 256), BF16),
            pltpu.VMEM((wins, kb, 256), BF16),
            pltpu.VMEM((n_sen, kb, 256), BF16),
            pltpu.VMEM((kb, 256), BF16),
            pltpu.VMEM((entries, 256), BF16),
            pltpu.VMEM((n_sky, entries), F32),
            pltpu.VMEM((n_sky, ROWS + META, 256), BF16),
            pltpu.VMEM((n_sky, ROWS + META, 256), BF16),
            pltpu.VMEM((wins, sens * n_sky, 256), BF16),
            pltpu.VMEM((sens * n_sky, 256), F32),
            pltpu.VMEM((n_sky, sens, 256), F32),
            pltpu.VMEM((sens, 256), F32),
            pltpu.VMEM((sens * n_sky, 256), F32),
            dma, dma((2,)), dma((2, nz)), dma((nz,)), dma((nz,)), dma((nz,)),
            dma((n_sky,)), dma((n_sky,)), dma((n_sky,)), dma((n_sky,)), dma((n_sky,)), dma((n_sky,)),
        ],
        compiler_params=pltpu.CompilerParams(collective_id=0, has_side_effects=True, vmem_limit_bytes=56 * 2**20),
    )(
        sky.T,
        jnp.transpose(daylight[0], (1, 0, 2)),
        bsdf[0],
        bsdf_ids,
        view[0].reshape(entries, bins),
        visible[0],
        counts,
    )
    result = lax.cond(
        flag[0, 0] > 0.0,
        lambda: general(sky, daylight, bsdf, bsdf_ids, view, visible, counts),
        lambda: out,
    )
    return result[None]


def solution(mesh):
    in_specs = (
        P(None, "sky"),
        P("sensor", "sky", None, None),
        P("sensor", None, None),
        P("sensor", "sky"),
        P("sensor", "sky", None, None),
        P("sensor", "sky", None),
        P("sensor", "sky"),
    )
    return jax.shard_map(body, mesh=mesh, in_specs=in_specs, out_specs=P("sensor", "sky", None), check_vma=False)
```

```python
import jax
import jax.numpy as jnp
from jax import lax
from jax.experimental import pallas as pl
from jax.experimental.pallas import tpu as pltpu
from jax.sharding import PartitionSpec as P

F32 = jnp.float32
BF16 = jnp.bfloat16
MESH = pl.DeviceIdType.MESH
ROWS = 48
FOLD = 16
STEP = 24
NOTE = 80
HUGE = 1e30


def up(n, m):
    return -(-n // m) * m


def iota(shape, dim):
    return lax.broadcasted_iota(jnp.int32, shape, dim)


def dot(a, b, dims=((1,), (0,))):
    return lax.dot_general(a, b, (dims, ((), ())), preferred_element_type=F32)


def fold(x, rows):
    parts = [x[g * rows : (g + 1) * rows] for g in range(x.shape[0] // rows)]
    return sum([p if g == 0 else pltpu.roll(p, g * STEP, 1) for g, p in enumerate(parts)])


def unfold(x, groups):
    return jnp.concatenate([x if g == 0 else pltpu.roll(x, 128 - g * STEP, 1) for g in range(groups)], axis=0)


def kernel(dims, first, sky_ref, day_hbm, bsdf_ref, ids_ref, view_ref, vis_ref, counts_ref, round_ref, out_ref, flag_ref,
           day, wide, days, mats, own, tail, store, skies, vpad, rank, send, got, dense, part, light, outs, ins, fown, fgot,
           day_sem, loc_sem, z_send, z_recv, s_send, s_recv, v_send, v_recv, p_send, p_recv, b_send, b_recv,
           f_send, f_recv, o_send, o_recv):
    n_sky, n_sen, bins, patches, wins, sens, slots, hours = dims
    nz = n_sen // 2
    kb = up(bins, 16)
    half = (kb + 32) // 2
    entries = sens * slots
    me = lax.axis_index("sky")
    mine = lax.axis_index("sensor")
    z, core = mine // 2, lax.rem(mine, 2)
    sibling = z * 2 + (1 - core)
    near, far = me, lax.rem(me + nz // 2, nz)

    def plane(shift, c):
        return lax.rem(z + shift + nz, nz) * 2 + c

    barrier = pltpu.get_barrier_semaphore()

    def greet(other_sky, other_sensor):
        pl.semaphore_signal(barrier, inc=1, device_id=(other_sky, other_sensor), device_id_type=MESH)

    def greet_sky(k, c):
        greet(lax.rem(me + k, n_sky), mine)
        return c

    lax.fori_loop(1, n_sky, greet_sky, 0)
    greet(me, sibling)
    if first:
        greet(me, plane(near, 1 - core))
    near_other, far_other = near != 0, far != 0

    @pl.when(near_other)
    def _():
        greet(me, plane(near, core))

    @pl.when(far_other)
    def _():
        greet(me, plane(far, core))

    day_copy = pltpu.make_async_copy(day_hbm, day, day_sem)
    day_copy.start()

    own[0:kb, :] = jnp.zeros((kb, 128), BF16)
    own[0:bins, :] = bsdf_ref[:, 0:128]
    tail[...] = jnp.zeros(tail.shape, F32)
    tail[0:bins, 0 : bins - 128] = bsdf_ref[:, 128:bins].astype(F32)
    own[kb : kb + 32, :] = fold(tail[...], 32).astype(BF16)
    skies[me] = jnp.zeros(skies.shape[1:], BF16)
    skies[me, :, 0:patches] = sky_ref[...]

    vis = vis_ref[...]
    owner = vis // wins
    local = vis - owner * wins
    spread = (lax.rem(iota((slots, entries), 1), slots) == iota((slots, entries), 0)).astype(BF16)
    sensor_of = iota((sens, entries), 1) // slots == iota((sens, entries), 0)

    def flat(x):
        return jnp.sum(jnp.where(sensor_of, dot(x.astype(F32).astype(BF16), spread), 0.0), axis=0, keepdims=True)

    owner_row, local_row = flat(owner), flat(local)
    slot_row = lax.rem(iota((1, entries), 1), slots).astype(F32)
    sens_row = (iota((1, entries), 1) // slots).astype(F32)
    counts = jnp.broadcast_to(counts_ref[...].astype(F32), (16, sens)).astype(BF16)
    count_row = dot(counts, sensor_of.astype(BF16))[0:1]
    live = slot_row < count_row
    goes = jnp.logical_and(iota((n_sky, entries), 0).astype(F32) == owner_row, live)
    goes_f = goes.astype(F32)
    earlier = (iota((entries, entries), 0) < iota((entries, entries), 1)).astype(BF16)
    ranks = dot(goes_f.astype(BF16), earlier) - (0 if first else (round_ref[0, 0] * ROWS).astype(F32))
    rank[...] = jnp.where(jnp.logical_and(goes, ranks >= 0.0), ranks, -1000.0)
    most = jnp.max(jnp.sum(goes_f, axis=1, keepdims=True), axis=0, keepdims=True)
    over = jnp.where(most > ROWS, 1.0, 0.0)

    pl.semaphore_wait(barrier, n_sky + (1 if first else 0) + near_other.astype(jnp.int32) + far_other.astype(jnp.int32))

    def along(i, to, c):
        return pltpu.make_async_remote_copy(
            src_ref=own.at[pl.ds(i * half, half)], dst_ref=store.at[core, me, i], send_sem=z_send.at[i],
            recv_sem=z_recv.at[i], device_id=(me, plane(-to, c)), device_id_type=MESH)

    def stay(i):
        return pltpu.make_async_copy(own.at[pl.ds(i * half, half)], store.at[core, me, i], z_recv.at[i])

    for i, to, other in ((0, near, near_other), (1, far, far_other)):

        @pl.when(other)
        def _(i=i, to=to):
            along(i, to, core).start()

        @pl.when(jnp.logical_not(other))
        def _(i=i):
            stay(i).start()

    def sky_copy(q, slot):
        return pltpu.make_async_remote_copy(
            src_ref=skies.at[slot], dst_ref=skies.at[slot], send_sem=s_send.at[q], recv_sem=s_recv.at[slot],
            device_id=(q, mine), device_id_type=MESH)

    vpad[...] = jnp.zeros(vpad.shape, BF16)
    vpad[:, 0:bins] = view_ref[...]
    note_row = iota((FOLD, entries), 0)
    notes = jnp.where(note_row == 0, local_row + 1.0, jnp.where(note_row == 1, sens_row, 0.0)).astype(BF16)
    place = (iota((128, entries), 0) - NOTE).astype(F32)
    at_flag = jnp.logical_and(iota((FOLD, 128), 0) == 2, iota((FOLD, 128), 1) >= NOTE)
    flag_note = jnp.where(at_flag, over, 0.0)

    def message(q, slot):
        return pltpu.make_async_remote_copy(
            src_ref=send.at[q], dst_ref=got.at[slot], send_sem=v_send.at[q], recv_sem=v_recv.at[slot],
            device_id=(q, mine), device_id_type=MESH)

    def pack(q):
        pick = (place == rank[pl.ds(q, 1), :]).astype(BF16)
        rows = dot(pick[NOTE : NOTE + ROWS], vpad[...])
        send[q, 0:ROWS, :] = rows[:, 0:128].astype(BF16)
        notes_at = dot(notes, pick, ((1,), (1,)))
        send[q, ROWS : ROWS + FOLD, :] = (fold(rows[:, 128:256], FOLD) + notes_at + flag_note).astype(BF16)

    def put(k, c):
        q = lax.rem(me + k, n_sky)
        pack(q)
        message(q, me).start()
        sky_copy(q, me).start()
        return c

    lax.fori_loop(1, n_sky, put, 0)
    pack(me)
    keep = pltpu.make_async_copy(send.at[me], got.at[me], loc_sem)
    keep.start()

    def in_plane(q, slot):
        return pltpu.make_async_remote_copy(
            src_ref=store.at[core, slot], dst_ref=store.at[core, slot], send_sem=p_send.at[q], recv_sem=p_recv.at[slot],
            device_id=(q, mine), device_id_type=MESH)

    def across(c, slot):
        return pltpu.make_async_remote_copy(
            src_ref=store.at[c, slot], dst_ref=store.at[c, slot], send_sem=b_send.at[slot], recv_sem=b_recv.at[slot],
            device_id=(me, sibling), device_id_type=MESH)

    for i in range(2):
        stay(i).wait()

    def put_plane(k, c):
        in_plane(lax.rem(me + k, n_sky), me).start()
        return c

    lax.fori_loop(1, n_sky, put_plane, 0)
    across(core, me).start()

    wide[1] = jnp.zeros(wide.shape[1:], F32)
    wide[0, bins * wins :, :] = jnp.zeros((wide.shape[1] - bins * wins, 128), F32)
    day_copy.wait()

    def widen(b, c):
        x = day[b].astype(F32)
        rows = pl.ds(pl.multiple_of(b * wins, 8), wins)
        wide[0, rows, :] = x[:, 0:128]
        wide[1, rows, 0 : patches - 128] = x[:, 128:patches]
        return c

    lax.fori_loop(0, bins, widen, 0, unroll=5 if bins % 5 == 0 else 1)

    def by_window(w, c):
        for i in range(2):
            days[w, :, i * 128 : i * 128 + 128] = wide[i, pl.ds(w, kb, stride=wins), :].astype(BF16)
        return c

    lax.fori_loop(0, wins, by_window, 0)

    keep.wait()

    def await_message(k, c):
        q = lax.rem(me + k, n_sky)
        message(q, q).wait_recv()
        return c

    lax.fori_loop(1, n_sky, await_message, 0)
    if first:
        flags = jnp.zeros((FOLD, 128), F32)
        for q in range(n_sky):
            flags = jnp.maximum(flags, got[q, ROWS : ROWS + FOLD, :].astype(F32))
        fown[...] = jnp.broadcast_to(flags[2:3, 127:128], fown.shape).astype(BF16)

        def flag_copy(i, c):
            return pltpu.make_async_remote_copy(
                src_ref=fown, dst_ref=fgot.at[i], send_sem=f_send.at[i], recv_sem=f_recv.at[i],
                device_id=(me, plane(-near, c)), device_id_type=MESH)

        flag_stay = pltpu.make_async_copy(fown, fgot.at[0], f_recv.at[0])

        @pl.when(near_other)
        def _():
            flag_copy(0, core).start()

        @pl.when(jnp.logical_not(near_other))
        def _():
            flag_stay.start()

        flag_copy(1, 1 - core).start()

    which = iota((wins * sens, ROWS), 0).astype(F32)

    def unpack(q, c):
        folded = got[q, ROWS : ROWS + FOLD, :].astype(F32)
        note = pltpu.roll(folded, 128 - NOTE, 1)[:, 0:ROWS]
        code = note[0:1] * float(sens) + note[1:2] - float(sens)
        pick = (which == code).astype(BF16)
        rows = jnp.concatenate([got[q, 0:ROWS, :], unfold(folded, ROWS // FOLD).astype(BF16)], axis=1)
        placed = dot(pick, rows).astype(BF16).reshape(wins, sens, 256)
        dense[:, pl.ds(pl.multiple_of(q * sens, sens), sens), :] = placed
        return c

    lax.fori_loop(0, n_sky, unpack, 0)

    def relay(k, c):
        q = lax.rem(me + k, n_sky)
        in_plane(q, q).wait_recv()
        across(core, q).start()
        return c

    lax.fori_loop(1, n_sky, relay, 0)

    def await_across(q, c):
        across(1 - core, q).wait_recv()
        return c

    lax.fori_loop(0, n_sky, await_across, 0)

    def through(w, c):
        table = ids_ref[0, w]
        away = table // 2 - z + nz
        a = store[table % 2, away % nz, 0]
        b = store[table % 2, (away + nz // 2) % nz, 1]
        ends = unfold(b[half - 32 :].astype(F32), kb // 32).astype(BF16)
        whole = jnp.concatenate([jnp.concatenate([a, b[0 : half - 32]], axis=0), ends], axis=1)
        mats[w] = dot(whole[:, 0:kb], days[w]).astype(BF16)
        return c

    lax.fori_loop(0, wins, through, 0, unroll=4)

    part[...] = jnp.zeros(part.shape, F32)
    group = 8 if wins % 8 == 0 else 1

    def gather(g, c):
        acc = part[...]
        for i in range(group):
            w = g * group + i
            acc = acc + dot(dense[w][:, 0:kb], mats[w])
        part[...] = acc
        return c

    lax.fori_loop(0, wins // group, gather, 0)

    def await_sky(k, c):
        q = lax.rem(me + k, n_sky)
        sky_copy(q, q).wait_recv()
        return c

    lax.fori_loop(1, n_sky, await_sky, 0)
    a = part[...]
    high = a.astype(BF16)
    low = (a - high.astype(F32)).astype(BF16)
    every = skies[...].reshape(n_sky * hours, 256)
    shares = dot(every, high, ((1,), (1,))) + dot(every, low, ((1,), (1,)))
    if first:
        flag_stay.wait()
        flag_copy(1, 1 - core).wait_recv()
        seen = jnp.maximum(fgot[0], fgot[1]).astype(F32)[0:1, 0:1]
        shares = jnp.where(seen > 0.0, HUGE, shares)
    light[...] = shares.reshape(light.shape)
    outs[...] = shares.astype(BF16).reshape(outs.shape)

    def share(q, slot):
        return pltpu.make_async_remote_copy(
            src_ref=outs.at[q], dst_ref=ins.at[slot], send_sem=o_send.at[q], recv_sem=o_recv.at[slot],
            device_id=(q, mine), device_id_type=MESH)

    def put_share(k, c):
        share(lax.rem(me + k, n_sky), me).start()
        return c

    lax.fori_loop(1, n_sky, put_share, 0)

    def add(k, total):
        q = lax.rem(me + k, n_sky)
        share(q, q).wait_recv()
        return total + ins[q].astype(F32)

    total = lax.fori_loop(1, n_sky, add, light[me])
    out_ref[...] = total
    flag_ref[0, 0] = jnp.max(total[0:8, 0:128])

    for i, other in enumerate((near_other, far_other)):

        @pl.when(other)
        def _(i=i):
            along(i, near, core).wait_send()

    if first:

        @pl.when(near_other)
        def _():
            flag_copy(0, core).wait_send()

        flag_copy(1, 1 - core).wait_send()

    def drain(k, c):
        q = lax.rem(me + k, n_sky)
        message(q, me).wait_send()
        sky_copy(q, me).wait_send()
        in_plane(q, me).wait_send()
        share(q, me).wait_send()
        return c

    lax.fori_loop(1, n_sky, drain, 0)

    def drain_across(q, c):
        across(core, q).wait_send()
        return c

    lax.fori_loop(0, n_sky, drain_across, 0)


def body(sky, daylight, bsdf, bsdf_ids, view, visible, counts):
    n_sky, n_sen = lax.axis_size("sky"), lax.axis_size("sensor")
    patches, hours = sky.shape
    _, wins, bins, _ = daylight.shape
    _, sens, slots, _ = view.shape
    kb, entries = up(bins, 32), sens * slots
    dims = (n_sky, n_sen, bins, patches, wins, sens, slots, hours)
    vmem, smem = pl.BlockSpec(memory_space=pltpu.VMEM), pl.BlockSpec(memory_space=pltpu.SMEM)
    dma, all_sens = pltpu.SemaphoreType.DMA, sens * n_sky
    args = (sky.T, jnp.transpose(daylight[0], (1, 0, 2)), bsdf[0], bsdf_ids, view[0].reshape(entries, bins), visible[0], counts)

    def call(first, number):
        def run(*refs):
            kernel(dims, first, *refs)

        return pl.pallas_call(
            run,
            out_shape=(jax.ShapeDtypeStruct((hours, all_sens), F32), jax.ShapeDtypeStruct((1, 1), F32)),
            in_specs=[vmem, pl.BlockSpec(memory_space=pl.ANY), vmem, smem, vmem, vmem, vmem, smem],
            out_specs=(vmem, smem),
            scratch_shapes=[
                pltpu.VMEM((bins, wins, patches), BF16),
                pltpu.VMEM((2, kb * wins, 128), F32),
                pltpu.VMEM((wins, kb, 256), BF16),
                pltpu.VMEM((wins, kb, 256), BF16),
                pltpu.VMEM((kb + 32, 128), BF16),
                pltpu.VMEM((kb, 128), F32),
                pltpu.VMEM((2, n_sky, 2, (kb + 32) // 2, 128), BF16),
                pltpu.VMEM((n_sky, hours, 256), BF16),
                pltpu.VMEM((entries, 256), BF16),
                pltpu.VMEM((n_sky, entries), F32),
                pltpu.VMEM((n_sky, ROWS + FOLD, 128), BF16),
                pltpu.VMEM((n_sky, ROWS + FOLD, 128), BF16),
                pltpu.VMEM((wins, all_sens, 256), BF16),
                pltpu.VMEM((all_sens, 256), F32),
                pltpu.VMEM((n_sky, hours, all_sens), F32),
                pltpu.VMEM((n_sky, hours, all_sens), BF16),
                pltpu.VMEM((n_sky, hours, all_sens), BF16),
                pltpu.VMEM((16, 128), BF16),
                pltpu.VMEM((2, 16, 128), BF16),
                dma, dma, dma((2,)), dma((2,)), dma((n_sky,)), dma((n_sky,)), dma((n_sky,)), dma((n_sky,)),
                dma((n_sky,)), dma((n_sky,)), dma((n_sky,)), dma((n_sky,)), dma((2,)), dma((2,)), dma((n_sky,)), dma((n_sky,)),
            ],
            compiler_params=pltpu.CompilerParams(
                collective_id=0 if first else 1, has_side_effects=True, vmem_limit_bytes=56 * 2**20),
        )(*args, jnp.reshape(number, (1, 1)).astype(jnp.int32))

    out, flag = call(True, jnp.zeros((), jnp.int32))

    def in_rounds():
        rounds = -(-entries // ROWS)
        return lax.fori_loop(0, rounds, lambda i, acc: acc + call(False, i)[0], jnp.zeros_like(out))

    return lax.cond(flag[0, 0] > HUGE / 1e6, in_rounds, lambda: out)[None]


def solution(mesh):
    in_specs = (
        P(None, "sky"),
        P("sensor", "sky", None, None),
        P("sensor", None, None),
        P("sensor", "sky"),
        P("sensor", "sky", None, None),
        P("sensor", "sky", None),
        P("sensor", "sky"),
    )
    return jax.shard_map(body, mesh=mesh, in_specs=in_specs, out_specs=P("sensor", "sky", None), check_vma=False)
```

```python
import jax
import jax.numpy as jnp
from jax import lax
from jax.experimental import pallas as pl
from jax.experimental.pallas import tpu as pltpu
from jax.sharding import PartitionSpec as P

F32 = jnp.float32
BF16 = jnp.bfloat16
MESH = pl.DeviceIdType.MESH
ROWS = 48
FOLD = 16
STEP = 24
NOTE = 80
HUGE = 1e30


def up(n, m):
    return -(-n // m) * m


def iota(shape, dim):
    return lax.broadcasted_iota(jnp.int32, shape, dim)


def dot(a, b, dims=((1,), (0,))):
    return lax.dot_general(a, b, (dims, ((), ())), preferred_element_type=F32)


def fold(x, rows):
    parts = [x[g * rows : (g + 1) * rows] for g in range(x.shape[0] // rows)]
    return sum([p if g == 0 else pltpu.roll(p, g * STEP, 1) for g, p in enumerate(parts)])


def unfold(x, groups):
    return jnp.concatenate([x if g == 0 else pltpu.roll(x, 128 - g * STEP, 1) for g in range(groups)], axis=0)


def kernel(dims, first, round_ref, sky_hbm, day_hbm, bsdf_hbm, ids_hbm, view_hbm, vis_hbm, counts_hbm, out_ref, flag_ref,
           sky_ref, day, bsdf_ref, ids_ref, view_ref, vis_ref, counts_ref, wide, days, mats, own, tail, store, skies, vpad, rank, send, got, dense, part, light, outs, ins, fown, fgot,
           in_sem, loc_sem, z_send, z_recv, v_send, v_recv, p_send, p_recv, b_send, b_recv,
           f_send, f_recv, o_send, o_recv):
    n_sky, n_sen, bins, patches, wins, sens, slots, hours = dims
    nz = n_sen // 2
    kb = up(bins, 16)
    half = (kb + 32) // 2
    entries = sens * slots
    me = lax.axis_index("sky")
    mine = lax.axis_index("sensor")
    z, core = mine // 2, lax.rem(mine, 2)
    sibling = z * 2 + (1 - core)
    near, far = me, lax.rem(me + nz // 2, nz)

    def plane(shift, c):
        return lax.rem(z + shift + nz, nz) * 2 + c

    load_sky, load_day, load_bsdf, load_ids, load_view, load_vis, load_counts = [
        pltpu.make_async_copy(src, dst, in_sem.at[i])
        for i, (src, dst) in enumerate((
            (sky_hbm, sky_ref), (day_hbm, day), (bsdf_hbm, bsdf_ref), (ids_hbm, ids_ref), (view_hbm, view_ref),
            (vis_hbm, vis_ref), (counts_hbm, counts_ref)))
    ]
    for load in (load_bsdf, load_vis, load_counts, load_view, load_sky, load_ids, load_day):
        load.start()
    barrier = pltpu.get_barrier_semaphore()

    def greet(other_sky, other_sensor):
        pl.semaphore_signal(barrier, inc=1, device_id=(other_sky, other_sensor), device_id_type=MESH)

    def greet_sky(k, c):
        greet(lax.rem(me + k, n_sky), mine)
        return c

    lax.fori_loop(1, n_sky, greet_sky, 0)
    greet(me, sibling)
    if first:
        greet(me, plane(near, 1 - core))
    near_other, far_other = near != 0, far != 0

    @pl.when(near_other)
    def _():
        greet(me, plane(near, core))

    @pl.when(far_other)
    def _():
        greet(me, plane(far, core))

    own[0:kb, :] = jnp.zeros((kb, 128), BF16)
    load_bsdf.wait()
    own[0:bins, :] = bsdf_ref[:, 0:128]
    tail[...] = jnp.zeros(tail.shape, F32)
    tail[0:bins, 0 : bins - 128] = bsdf_ref[:, 128:bins].astype(F32)
    own[kb : kb + 32, :] = fold(tail[...], 32).astype(BF16)
    ins[me] = jnp.zeros(ins.shape[1:], BF16)

    load_vis.wait()
    load_counts.wait()
    vis = vis_ref[...]
    owner = vis // wins
    local = vis - owner * wins
    spread = (lax.rem(iota((slots, entries), 1), slots) == iota((slots, entries), 0)).astype(BF16)
    sensor_of = iota((sens, entries), 1) // slots == iota((sens, entries), 0)

    def flat(x):
        return jnp.sum(jnp.where(sensor_of, dot(x.astype(F32).astype(BF16), spread), 0.0), axis=0, keepdims=True)

    owner_row, local_row = flat(owner), flat(local)
    slot_row = lax.rem(iota((1, entries), 1), slots).astype(F32)
    sens_row = (iota((1, entries), 1) // slots).astype(F32)
    counts = jnp.broadcast_to(counts_ref[...].astype(F32), (16, sens)).astype(BF16)
    count_row = dot(counts, sensor_of.astype(BF16))[0:1]
    live = slot_row < count_row
    goes = jnp.logical_and(iota((n_sky, entries), 0).astype(F32) == owner_row, live)
    goes_f = goes.astype(F32)
    earlier = (iota((entries, entries), 0) < iota((entries, entries), 1)).astype(BF16)
    ranks = dot(goes_f.astype(BF16), earlier) - (0 if first else (round_ref[0, 0] * ROWS).astype(F32))
    rank[...] = jnp.where(jnp.logical_and(goes, ranks >= 0.0), ranks, -1000.0)
    most = jnp.max(jnp.sum(goes_f, axis=1, keepdims=True), axis=0, keepdims=True)
    over = jnp.where(most > ROWS, 1.0, 0.0)

    pl.semaphore_wait(barrier, n_sky + (1 if first else 0) + near_other.astype(jnp.int32) + far_other.astype(jnp.int32))

    def along(i, to, c):
        return pltpu.make_async_remote_copy(
            src_ref=own.at[pl.ds(i * half, half)], dst_ref=store.at[core, me, i], send_sem=z_send.at[i],
            recv_sem=z_recv.at[i], device_id=(me, plane(-to, c)), device_id_type=MESH)

    def stay(i):
        return pltpu.make_async_copy(own.at[pl.ds(i * half, half)], store.at[core, me, i], z_recv.at[i])

    for i, to, other in ((0, near, near_other), (1, far, far_other)):

        @pl.when(other)
        def _(i=i, to=to):
            along(i, to, core).start()

        @pl.when(jnp.logical_not(other))
        def _(i=i):
            stay(i).start()

    sky_at = ROWS + FOLD
    load_view.wait()
    load_sky.wait()
    tail[0:hours, :] = jnp.zeros((hours, 128), F32)
    tail[0:hours, 0 : patches - 128] = sky_ref[:, 128:patches].astype(F32)
    sky_ends = fold(tail[0:hours, :], FOLD).astype(BF16)
    vpad[...] = jnp.zeros(vpad.shape, BF16)
    vpad[:, 0:bins] = view_ref[...]
    note_row = iota((FOLD, entries), 0)
    notes = jnp.where(note_row == 0, local_row + 1.0, jnp.where(note_row == 1, sens_row, 0.0)).astype(BF16)
    place = (iota((128, entries), 0) - NOTE).astype(F32)
    at_flag = jnp.logical_and(iota((FOLD, 128), 0) == 2, iota((FOLD, 128), 1) >= NOTE)
    flag_note = jnp.where(at_flag, over, 0.0)

    def message(q):
        return pltpu.make_async_remote_copy(
            src_ref=send.at[q], dst_ref=got.at[me], send_sem=v_send, recv_sem=v_recv,
            device_id=(q, mine), device_id_type=MESH)

    def all_of(ref, sem, n):
        return pltpu.make_async_copy(ref.at[pl.ds(0, n)], ref.at[pl.ds(0, n)], sem)

    def pack(q, c):
        pick = (place == rank[pl.ds(q, 1), :]).astype(BF16)
        rows = dot(pick[NOTE : NOTE + ROWS], vpad[...])
        send[q, 0:ROWS, :] = rows[:, 0:128].astype(BF16)
        notes_at = dot(notes, pick, ((1,), (1,)))
        send[q, ROWS : ROWS + FOLD, :] = (fold(rows[:, 128:256], FOLD) + notes_at + flag_note).astype(BF16)
        send[q, sky_at : sky_at + hours, :] = sky_ref[:, 0:128]
        send[q, sky_at + hours :, :] = sky_ends
        return c

    lax.fori_loop(0, n_sky, pack, 0, unroll=4 if n_sky % 4 == 0 else 1)

    def put(k, c):
        message(lax.rem(me + k, n_sky)).start()
        return c

    lax.fori_loop(1, n_sky, put, 0)
    keep = pltpu.make_async_copy(send.at[me], got.at[me], loc_sem)
    keep.start()

    def in_plane(q, slot):
        return pltpu.make_async_remote_copy(
            src_ref=store.at[core, slot], dst_ref=store.at[core, slot], send_sem=p_send, recv_sem=p_recv.at[slot],
            device_id=(q, mine), device_id_type=MESH)

    def across(c, slot):
        return pltpu.make_async_remote_copy(
            src_ref=store.at[c, slot], dst_ref=store.at[c, slot], send_sem=b_send, recv_sem=b_recv,
            device_id=(me, sibling), device_id_type=MESH)

    for i in range(2):
        stay(i).wait()

    def put_plane(k, c):
        in_plane(lax.rem(me + k, n_sky), me).start()
        return c

    lax.fori_loop(1, n_sky, put_plane, 0)
    across(core, me).start()

    wide[1] = jnp.zeros(wide.shape[1:], F32)
    wide[0, bins * wins :, :] = jnp.zeros((wide.shape[1] - bins * wins, 128), F32)
    load_day.wait()

    def widen(b, c):
        x = day[b].astype(F32)
        rows = pl.ds(pl.multiple_of(b * wins, 8), wins)
        wide[0, rows, :] = x[:, 0:128]
        wide[1, rows, 0 : patches - 128] = x[:, 128:patches]
        return c

    lax.fori_loop(0, bins, widen, 0, unroll=5 if bins % 5 == 0 else 1)

    def by_window(w, c):
        for i in range(2):
            days[w, :, i * 128 : i * 128 + 128] = wide[i, pl.ds(w, kb, stride=wins), :].astype(BF16)
        return c

    lax.fori_loop(0, wins, by_window, 0)

    keep.wait()

    all_of(got, v_recv, n_sky - 1).wait()
    if first:
        flags = jnp.zeros((FOLD, 128), F32)
        for q in range(n_sky):
            flags = jnp.maximum(flags, got[q, ROWS : ROWS + FOLD, :].astype(F32))
        fown[...] = jnp.broadcast_to(flags[2:3, 127:128], fown.shape).astype(BF16)

        def flag_copy(i, c):
            return pltpu.make_async_remote_copy(
                src_ref=fown, dst_ref=fgot.at[i], send_sem=f_send.at[i], recv_sem=f_recv.at[i],
                device_id=(me, plane(-near, c)), device_id_type=MESH)

        flag_stay = pltpu.make_async_copy(fown, fgot.at[0], f_recv.at[0])

        @pl.when(near_other)
        def _():
            flag_copy(0, core).start()

        @pl.when(jnp.logical_not(near_other))
        def _():
            flag_stay.start()

        flag_copy(1, 1 - core).start()

    which = iota((wins * sens, ROWS), 0).astype(F32)

    def unpack(q, c):
        folded = got[q, ROWS : ROWS + FOLD, :].astype(F32)
        note = pltpu.roll(folded, 128 - NOTE, 1)[:, 0:ROWS]
        code = note[0:1] * float(sens) + note[1:2] - float(sens)
        pick = (which == code).astype(BF16)
        rows = jnp.concatenate([got[q, 0:ROWS, :], unfold(folded, ROWS // FOLD).astype(BF16)], axis=1)
        placed = dot(pick, rows).astype(BF16).reshape(wins, sens, 256)
        dense[:, pl.ds(pl.multiple_of(q * sens, sens), sens), :] = placed
        skies[q, :, 0:128] = got[q, sky_at : sky_at + hours, :]
        skies[q, :, 128:256] = unfold(got[q, sky_at + hours :, :].astype(F32), hours // FOLD).astype(BF16)
        return c

    lax.fori_loop(0, n_sky, unpack, 0)

    def relay(k, c):
        q = lax.rem(me + k, n_sky)
        in_plane(q, q).wait_recv()
        across(core, q).start()
        return c

    lax.fori_loop(1, n_sky, relay, 0)

    load_ids.wait()
    all_of(store.at[1 - core], b_recv, n_sky).wait()

    def through(w, c):
        table = ids_ref[0, w]
        away = table // 2 - z + nz
        a = store[table % 2, away % nz, 0]
        b = store[table % 2, (away + nz // 2) % nz, 1]
        ends = unfold(b[half - 32 :].astype(F32), kb // 32).astype(BF16)
        whole = jnp.concatenate([jnp.concatenate([a, b[0 : half - 32]], axis=0), ends], axis=1)
        mats[w] = dot(whole[:, 0:kb], days[w]).astype(BF16)
        return c

    lax.fori_loop(0, wins, through, 0, unroll=8 if wins % 8 == 0 else 1)

    part[...] = jnp.zeros(part.shape, F32)
    group = 8 if wins % 8 == 0 else 1

    def gather(g, c):
        acc = part[...]
        for i in range(group):
            w = g * group + i
            acc = acc + dot(dense[w][:, 0:kb], mats[w])
        part[...] = acc
        return c

    lax.fori_loop(0, wins // group, gather, 0)

    a = part[...]
    high = a.astype(BF16)
    low = (a - high.astype(F32)).astype(BF16)
    every = skies[...].reshape(n_sky * hours, 256)
    shares = dot(every, high, ((1,), (1,))) + dot(every, low, ((1,), (1,)))
    if first:
        flag_stay.wait()
        flag_copy(1, 1 - core).wait_recv()
        seen = jnp.maximum(fgot[0], fgot[1]).astype(F32)[0:1, 0:1]
        shares = jnp.where(seen > 0.0, HUGE, shares)
    light[...] = shares.reshape(light.shape)
    outs[...] = shares.astype(BF16).reshape(outs.shape)

    def put_share(k, c):
        q = lax.rem(me + k, n_sky)
        pltpu.make_async_remote_copy(
            src_ref=outs.at[q], dst_ref=ins.at[me], send_sem=o_send, recv_sem=o_recv,
            device_id=(q, mine), device_id_type=MESH).start()
        return c

    lax.fori_loop(1, n_sky, put_share, 0)

    all_of(ins, o_recv, n_sky - 1).wait()
    total = light[me]
    for q in range(n_sky):
        total = total + ins[q].astype(F32)
    out_ref[...] = total
    flag_ref[0, 0] = jnp.max(total[0:8, 0:128])

    for i, other in enumerate((near_other, far_other)):

        @pl.when(other)
        def _(i=i):
            along(i, near, core).wait_send()

    if first:

        @pl.when(near_other)
        def _():
            flag_copy(0, core).wait_send()

        flag_copy(1, 1 - core).wait_send()

    all_of(send, v_send, n_sky - 1).wait()
    all_of(store.at[core], p_send, n_sky - 1).wait()
    all_of(store.at[core], b_send, n_sky).wait()
    all_of(outs, o_send, n_sky - 1).wait()


def body(sky, daylight, bsdf, bsdf_ids, view, visible, counts):
    n_sky, n_sen = lax.axis_size("sky"), lax.axis_size("sensor")
    patches, hours = sky.shape
    _, wins, bins, _ = daylight.shape
    _, sens, slots, _ = view.shape
    kb, entries = up(bins, 32), sens * slots
    dims = (n_sky, n_sen, bins, patches, wins, sens, slots, hours)
    vmem, smem = pl.BlockSpec(memory_space=pltpu.VMEM), pl.BlockSpec(memory_space=pltpu.SMEM)
    dma, all_sens = pltpu.SemaphoreType.DMA, sens * n_sky
    args = (sky.T, jnp.transpose(daylight[0], (1, 0, 2)), bsdf[0], bsdf_ids, view[0].reshape(entries, bins), visible[0], counts)

    def call(first, number):
        def run(*refs):
            if first:
                refs = (None,) + refs
            kernel(dims, first, *refs)

        return pl.pallas_call(
            run,
            out_shape=(jax.ShapeDtypeStruct((hours, all_sens), F32), jax.ShapeDtypeStruct((1, 1), F32)),
            in_specs=([] if first else [smem]) + [pl.BlockSpec(memory_space=pl.ANY)] * 7,
            out_specs=(vmem, smem),
            scratch_shapes=[
                pltpu.VMEM((hours, patches), BF16),
                pltpu.VMEM((bins, wins, patches), BF16),
                pltpu.VMEM((bins, bins), BF16),
                pltpu.SMEM((1, wins), jnp.int32),
                pltpu.VMEM((entries, bins), BF16),
                pltpu.VMEM((sens, slots), jnp.int32),
                pltpu.VMEM((1, sens), jnp.int32),
                pltpu.VMEM((2, kb * wins, 128), F32),
                pltpu.VMEM((wins, kb, 256), BF16),
                pltpu.VMEM((wins, kb, 256), BF16),
                pltpu.VMEM((kb + 32, 128), BF16),
                pltpu.VMEM((kb, 128), F32),
                pltpu.VMEM((2, n_sky, 2, (kb + 32) // 2, 128), BF16),
                pltpu.VMEM((n_sky, hours, 256), BF16),
                pltpu.VMEM((entries, 256), BF16),
                pltpu.VMEM((n_sky, entries), F32),
                pltpu.VMEM((n_sky, ROWS + 2 * FOLD + hours, 128), BF16),
                pltpu.VMEM((n_sky, ROWS + 2 * FOLD + hours, 128), BF16),
                pltpu.VMEM((wins, all_sens, 256), BF16),
                pltpu.VMEM((all_sens, 256), F32),
                pltpu.VMEM((n_sky, hours, all_sens), F32),
                pltpu.VMEM((n_sky, hours, all_sens), BF16),
                pltpu.VMEM((n_sky, hours, all_sens), BF16),
                pltpu.VMEM((16, 128), BF16),
                pltpu.VMEM((2, 16, 128), BF16),
                dma((7,)), dma, dma((2,)), dma((2,)), dma, dma, dma, dma((n_sky,)), dma, dma, dma((2,)), dma((2,)), dma, dma,
            ],
            compiler_params=pltpu.CompilerParams(
                collective_id=0 if first else 1, has_side_effects=True, vmem_limit_bytes=56 * 2**20),
        )(*(() if first else (jnp.reshape(number, (1, 1)).astype(jnp.int32),)), *args)

    out, flag = call(True, 0)

    def in_rounds():
        rounds = -(-entries // ROWS)
        return lax.fori_loop(0, rounds, lambda i, acc: acc + call(False, i)[0], jnp.zeros_like(out))

    return lax.cond(flag[0, 0] > HUGE / 1e6, in_rounds, lambda: out)[None]


def solution(mesh):
    in_specs = (
        P(None, "sky"),
        P("sensor", "sky", None, None),
        P("sensor", None, None),
        P("sensor", "sky"),
        P("sensor", "sky", None, None),
        P("sensor", "sky", None),
        P("sensor", "sky"),
    )
    return jax.shard_map(body, mesh=mesh, in_specs=in_specs, out_specs=P("sensor", "sky", None), check_vma=False)
```

```python
import jax
import jax.numpy as jnp
from jax import lax
from jax.experimental import pallas as pl
from jax.experimental.pallas import tpu as pltpu
from jax.sharding import PartitionSpec as P

F32 = jnp.float32
BF16 = jnp.bfloat16
MESH = pl.DeviceIdType.MESH
ROWS = 48
FOLD = 16
STEP = 24
NOTE = 80
HUGE = 1e30


def up(n, m):
    return -(-n // m) * m


def iota(shape, dim):
    return lax.broadcasted_iota(jnp.int32, shape, dim)


def dot(a, b, dims=((1,), (0,))):
    return lax.dot_general(a, b, (dims, ((), ())), preferred_element_type=F32)


def fold(x, rows):
    parts = [x[g * rows : (g + 1) * rows] for g in range(x.shape[0] // rows)]
    return sum([p if g == 0 else pltpu.roll(p, g * STEP, 1) for g, p in enumerate(parts)])


def unfold(x, groups):
    return jnp.concatenate([x if g == 0 else pltpu.roll(x, 128 - g * STEP, 1) for g in range(groups)], axis=0)


def kernel(dims, first, round_ref, sky_hbm, day_hbm, bsdf_hbm, ids_hbm, view_hbm, vis_hbm, counts_hbm, out_ref, flag_ref,
           sky_ref, day, bsdf_ref, ids_ref, view_ref, vis_ref, counts_ref, wide, days, mats, own, tail, store, hours_in, skies, vpad, rank, send, got, dense, light, outs, ins, fown, fgot,
           in_sem, loc_sem, z_send, z_recv, s_send, s_recv, v_send, v_recv, p_send, p_recv, b_send, b_recv,
           f_send, f_recv, o_send, o_recv):
    n_sky, n_sen, bins, patches, wins, sens, slots, hours = dims
    nz = n_sen // 2
    kb = up(bins, 16)
    half = (kb + 32) // 2
    entries = sens * slots
    me = lax.axis_index("sky")
    mine = lax.axis_index("sensor")
    z, core = mine // 2, lax.rem(mine, 2)
    sibling = z * 2 + (1 - core)
    near, far = me, lax.rem(me + nz // 2, nz)

    def plane(shift, c):
        return lax.rem(z + shift + nz, nz) * 2 + c

    load_sky, load_day, load_bsdf, load_ids, load_view, load_vis, load_counts = [
        pltpu.make_async_copy(src, dst, in_sem.at[i])
        for i, (src, dst) in enumerate((
            (sky_hbm, sky_ref), (day_hbm, day), (bsdf_hbm, bsdf_ref), (ids_hbm, ids_ref), (view_hbm, view_ref),
            (vis_hbm, vis_ref), (counts_hbm, counts_ref)))
    ]
    def all_of(ref, sem, n):
        return pltpu.make_async_copy(ref.at[pl.ds(0, n)], ref.at[pl.ds(0, n)], sem)

    barrier = pltpu.get_barrier_semaphore()

    def greet(other_sky, other_sensor):
        pl.semaphore_signal(barrier, inc=1, device_id=(other_sky, other_sensor), device_id_type=MESH)

    def greet_sky(k, c):
        greet(lax.rem(me + k, n_sky), mine)
        return c

    near_other, far_other = near != 0, far != 0

    @pl.when(near_other)
    def _():
        greet(me, plane(near, core))

    @pl.when(far_other)
    def _():
        greet(me, plane(far, core))

    if first:
        greet(me, plane(near, 1 - core))
    lax.fori_loop(1, n_sky, greet_sky, 0)
    greet(me, sibling)

    for load in (load_bsdf, load_vis, load_counts, load_view, load_sky, load_ids, load_day):
        load.start()

    own[0:kb, :] = jnp.zeros((kb, 128), BF16)
    load_bsdf.wait()
    own[0:bins, :] = bsdf_ref[:, 0:128]
    tail[...] = jnp.zeros(tail.shape, F32)
    tail[0:bins, 0 : bins - 128] = bsdf_ref[:, 128:bins].astype(F32)
    own[kb : kb + 32, :] = fold(tail[...], 32).astype(BF16)
    ins[me] = jnp.zeros(ins.shape[1:], BF16)

    load_vis.wait()
    load_counts.wait()
    vis = vis_ref[...]
    owner = vis // wins
    local = vis - owner * wins
    spread = (lax.rem(iota((slots, entries), 1), slots) == iota((slots, entries), 0)).astype(BF16)
    sensor_of = iota((sens, entries), 1) // slots == iota((sens, entries), 0)

    def flat(x):
        return jnp.sum(jnp.where(sensor_of, dot(x.astype(F32).astype(BF16), spread), 0.0), axis=0, keepdims=True)

    owner_row, local_row = flat(owner), flat(local)
    slot_row = lax.rem(iota((1, entries), 1), slots).astype(F32)
    sens_row = (iota((1, entries), 1) // slots).astype(F32)
    counts = jnp.broadcast_to(counts_ref[...].astype(F32), (16, sens)).astype(BF16)
    count_row = dot(counts, sensor_of.astype(BF16))[0:1]
    live = slot_row < count_row
    goes = jnp.logical_and(iota((n_sky, entries), 0).astype(F32) == owner_row, live)
    goes_f = goes.astype(F32)
    earlier = (iota((entries, entries), 0) < iota((entries, entries), 1)).astype(BF16)
    ranks = dot(goes_f.astype(BF16), earlier) - (0 if first else (round_ref[0, 0] * ROWS).astype(F32))
    rank[...] = jnp.where(jnp.logical_and(goes, ranks >= 0.0), ranks, -1000.0)
    most = jnp.max(jnp.sum(goes_f, axis=1, keepdims=True), axis=0, keepdims=True)
    over = jnp.where(most > ROWS, 1.0, 0.0)

    pl.semaphore_wait(barrier, n_sky + (1 if first else 0) + near_other.astype(jnp.int32) + far_other.astype(jnp.int32))

    def along(i, to, c):
        return pltpu.make_async_remote_copy(
            src_ref=own.at[pl.ds(i * half, half)], dst_ref=store.at[core, me, i], send_sem=z_send.at[i],
            recv_sem=z_recv.at[i], device_id=(me, plane(-to, c)), device_id_type=MESH)

    def stay(i):
        return pltpu.make_async_copy(own.at[pl.ds(i * half, half)], store.at[core, me, i], z_recv.at[i])

    for i, to, other in ((0, near, near_other), (1, far, far_other)):

        @pl.when(other)
        def _(i=i, to=to):
            along(i, to, core).start()

        @pl.when(jnp.logical_not(other))
        def _(i=i):
            stay(i).start()

    load_view.wait()
    vpad[...] = jnp.zeros(vpad.shape, BF16)
    vpad[:, 0:bins] = view_ref[...]
    note_row = iota((FOLD, entries), 0)
    notes = jnp.where(note_row == 0, local_row + 1.0, jnp.where(note_row == 1, sens_row, 0.0)).astype(BF16)
    place = (iota((128, entries), 0) - NOTE).astype(F32)
    at_flag = jnp.logical_and(iota((FOLD, 128), 0) == 2, iota((FOLD, 128), 1) >= NOTE)
    flag_note = jnp.where(at_flag, over, 0.0)

    def message(q):
        return pltpu.make_async_remote_copy(
            src_ref=send.at[q], dst_ref=got.at[me], send_sem=v_send, recv_sem=v_recv,
            device_id=(q, mine), device_id_type=MESH)

    def pack(q, c):
        pick = (place == rank[pl.ds(q, 1), :]).astype(BF16)
        rows = dot(pick[NOTE : NOTE + ROWS], vpad[...])
        send[q, 0:ROWS, :] = rows[:, 0:128].astype(BF16)
        notes_at = dot(notes, pick, ((1,), (1,)))
        send[q, ROWS : ROWS + FOLD, :] = (fold(rows[:, 128:256], FOLD) + notes_at + flag_note).astype(BF16)
        return c

    lax.fori_loop(0, n_sky, pack, 0, unroll=4 if n_sky % 4 == 0 else 1)

    def put(k, c):
        message(lax.rem(me + k, n_sky)).start()
        return c

    lax.fori_loop(1, n_sky, put, 0)
    keep = pltpu.make_async_copy(send.at[me], got.at[me], loc_sem)
    keep.start()

    def in_plane(q, slot):
        return pltpu.make_async_remote_copy(
            src_ref=store.at[core, slot], dst_ref=store.at[core, slot], send_sem=p_send, recv_sem=p_recv.at[slot],
            device_id=(q, mine), device_id_type=MESH)

    def across(c, slot):
        return pltpu.make_async_remote_copy(
            src_ref=store.at[c, slot], dst_ref=store.at[c, slot], send_sem=b_send, recv_sem=b_recv,
            device_id=(me, sibling), device_id_type=MESH)

    for i in range(2):
        stay(i).wait()

    def put_plane(k, c):
        in_plane(lax.rem(me + k, n_sky), me).start()
        return c

    lax.fori_loop(1, n_sky, put_plane, 0)
    across(core, me).start()

    load_sky.wait()
    tail[0:hours, :] = jnp.zeros((hours, 128), F32)
    tail[0:hours, 0 : patches - 128] = sky_ref[:, 128:patches].astype(F32)
    hours_in[me, 0:hours, :] = sky_ref[:, 0:128]
    hours_in[me, hours:, :] = fold(tail[0:hours, :], FOLD).astype(BF16)

    def put_hours(k, c):
        pltpu.make_async_remote_copy(
            src_ref=hours_in.at[me], dst_ref=hours_in.at[me], send_sem=s_send, recv_sem=s_recv,
            device_id=(lax.rem(me + k, n_sky), mine), device_id_type=MESH).start()
        return c

    lax.fori_loop(1, n_sky, put_hours, 0)

    wide[1] = jnp.zeros(wide.shape[1:], F32)
    wide[0, bins * wins :, :] = jnp.zeros((wide.shape[1] - bins * wins, 128), F32)
    load_day.wait()

    def widen(b, c):
        x = day[b].astype(F32)
        rows = pl.ds(pl.multiple_of(b * wins, 8), wins)
        wide[0, rows, :] = x[:, 0:128]
        wide[1, rows, 0 : patches - 128] = x[:, 128:patches]
        return c

    lax.fori_loop(0, bins, widen, 0, unroll=5 if bins % 5 == 0 else 1)

    def by_window(w, c):
        for i in range(2):
            days[w, :, i * 128 : i * 128 + 128] = wide[i, pl.ds(w, kb, stride=wins), :].astype(BF16)
        return c

    lax.fori_loop(0, wins, by_window, 0)

    keep.wait()

    all_of(got, v_recv, n_sky - 1).wait()
    if first:
        flags = jnp.zeros((FOLD, 128), F32)
        for q in range(n_sky):
            flags = jnp.maximum(flags, got[q, ROWS : ROWS + FOLD, :].astype(F32))
        fown[...] = jnp.broadcast_to(flags[2:3, 127:128], fown.shape).astype(BF16)

        def flag_copy(i, c):
            return pltpu.make_async_remote_copy(
                src_ref=fown, dst_ref=fgot.at[i], send_sem=f_send.at[i], recv_sem=f_recv.at[i],
                device_id=(me, plane(-near, c)), device_id_type=MESH)

        flag_stay = pltpu.make_async_copy(fown, fgot.at[0], f_recv.at[0])

        @pl.when(near_other)
        def _():
            flag_copy(0, core).start()

        @pl.when(jnp.logical_not(near_other))
        def _():
            flag_stay.start()

        flag_copy(1, 1 - core).start()

    which = iota((wins // 4 * sens, ROWS), 0).astype(F32)
    keep_tail = iota((ROWS, 128), 1) < kb - 128

    def unpack(q, c):
        folded = got[q, ROWS : ROWS + FOLD, :].astype(F32)
        note = pltpu.roll(folded, 128 - NOTE, 1)[:, 0:ROWS]
        window = note[0:1] - 1.0
        four = jnp.floor(window * 0.25)
        place_in = window - 4.0 * four
        target = four * float(sens) + note[1:2]
        ends = jnp.where(keep_tail, unfold(folded, ROWS // FOLD), 0.0)
        rows = jnp.concatenate([got[q, 0:ROWS, :].astype(F32), ends], axis=1)
        parts = []
        for m in range(4):
            pick = (which == jnp.where(place_in == float(m), target, -1.0)).astype(BF16)
            moved = rows if m == 0 else pltpu.roll(rows, m * (kb - 128), 1)
            parts.append(dot(pick, moved.astype(BF16)))
        at = pl.ds(pl.multiple_of(q * sens, sens), sens)
        for t in range(5):
            tile = parts[t][:, 0:128] if t < 4 else parts[3][:, 128:256]
            if 0 < t < 4:
                tile = tile + parts[t - 1][:, 128:256]
            tile = tile.astype(BF16).reshape(wins // 8, 2, sens, 128)
            for h in range(2):
                dense[:, at, h * 4 * kb + t * 128 : h * 4 * kb + t * 128 + 128] = tile[:, h]
        return c

    lax.fori_loop(0, n_sky, unpack, 0, unroll=2 if n_sky % 2 == 0 else 1)

    def relay(k, c):
        q = lax.rem(me + k, n_sky)
        in_plane(q, q).wait_recv()
        across(core, q).start()
        return c

    lax.fori_loop(1, n_sky, relay, 0)

    all_of(hours_in, s_recv, n_sky - 1).wait()

    def unfold_hours(q, c):
        skies[q, :, 0:128] = hours_in[q, 0:hours, :]
        skies[q, :, 128:256] = unfold(hours_in[q, hours:, :].astype(F32), hours // FOLD).astype(BF16)
        return c

    lax.fori_loop(0, n_sky, unfold_hours, 0, unroll=4 if n_sky % 4 == 0 else 1)
    load_ids.wait()
    all_of(store.at[1 - core], b_recv, n_sky).wait()

    def through(w, c):
        table = ids_ref[0, w]
        away = table // 2 - z + nz
        a = store[table % 2, away % nz, 0]
        b = store[table % 2, (away + nz // 2) % nz, 1]
        ends = unfold(b[half - 32 :].astype(F32), kb // 32).astype(BF16)
        whole = jnp.concatenate([jnp.concatenate([a, b[0 : half - 32]], axis=0), ends], axis=1)
        mats[w] = dot(whole[:, 0:kb], days[w]).astype(BF16)
        return c

    lax.fori_loop(0, wins, through, 0, unroll=8 if wins % 8 == 0 else 1)

    a = jnp.zeros((sens * n_sky, 256), F32)
    for g in range(wins // 8):
        a = a + dot(dense[g], mats[g * 8 : g * 8 + 8].reshape(8 * kb, 256))

    high = a.astype(BF16)
    low = (a - high.astype(F32)).astype(BF16)
    every = skies[...].reshape(n_sky * hours, 256)
    shares = dot(every, high, ((1,), (1,))) + dot(every, low, ((1,), (1,)))
    if first:
        flag_stay.wait()
        flag_copy(1, 1 - core).wait_recv()
        seen = jnp.maximum(fgot[0], fgot[1]).astype(F32)[0:1, 0:1]
        shares = jnp.where(seen > 0.0, HUGE, shares)
    light[...] = shares.reshape(light.shape)
    outs[...] = shares.astype(BF16).reshape(outs.shape)

    def put_share(k, c):
        q = lax.rem(me + k, n_sky)
        pltpu.make_async_remote_copy(
            src_ref=outs.at[q], dst_ref=ins.at[me], send_sem=o_send, recv_sem=o_recv,
            device_id=(q, mine), device_id_type=MESH).start()
        return c

    lax.fori_loop(1, n_sky, put_share, 0)

    all_of(ins, o_recv, n_sky - 1).wait()
    total = light[me]
    for q in range(n_sky):
        total = total + ins[q].astype(F32)
    out_ref[...] = total
    flag_ref[0, 0] = jnp.max(total[0:8, 0:128])

    for i, other in enumerate((near_other, far_other)):

        @pl.when(other)
        def _(i=i):
            along(i, near, core).wait_send()

    if first:

        @pl.when(near_other)
        def _():
            flag_copy(0, core).wait_send()

        flag_copy(1, 1 - core).wait_send()

    all_of(send, v_send, n_sky - 1).wait()
    all_of(hours_in, s_send, n_sky - 1).wait()
    all_of(store.at[core], p_send, n_sky - 1).wait()
    all_of(store.at[core], b_send, n_sky).wait()
    all_of(outs, o_send, n_sky - 1).wait()


def body(sky, daylight, bsdf, bsdf_ids, view, visible, counts):
    n_sky, n_sen = lax.axis_size("sky"), lax.axis_size("sensor")
    patches, hours = sky.shape
    _, wins, bins, _ = daylight.shape
    _, sens, slots, _ = view.shape
    kb, entries = up(bins, 32), sens * slots
    dims = (n_sky, n_sen, bins, patches, wins, sens, slots, hours)
    vmem, smem = pl.BlockSpec(memory_space=pltpu.VMEM), pl.BlockSpec(memory_space=pltpu.SMEM)
    dma, all_sens = pltpu.SemaphoreType.DMA, sens * n_sky
    args = (sky.T, jnp.transpose(daylight[0], (1, 0, 2)), bsdf[0], bsdf_ids, view[0].reshape(entries, bins), visible[0], counts)

    def call(first, number):
        def run(*refs):
            if first:
                refs = (None,) + refs
            kernel(dims, first, *refs)

        return pl.pallas_call(
            run,
            out_shape=(jax.ShapeDtypeStruct((hours, all_sens), F32), jax.ShapeDtypeStruct((1, 1), F32)),
            in_specs=([] if first else [smem]) + [pl.BlockSpec(memory_space=pl.ANY)] * 7,
            out_specs=(vmem, smem),
            scratch_shapes=[
                pltpu.VMEM((hours, patches), BF16),
                pltpu.VMEM((bins, wins, patches), BF16),
                pltpu.VMEM((bins, bins), BF16),
                pltpu.SMEM((1, wins), jnp.int32),
                pltpu.VMEM((entries, bins), BF16),
                pltpu.VMEM((sens, slots), jnp.int32),
                pltpu.VMEM((1, sens), jnp.int32),
                pltpu.VMEM((2, kb * wins, 128), F32),
                pltpu.VMEM((wins, kb, 256), BF16),
                pltpu.VMEM((wins, kb, 256), BF16),
                pltpu.VMEM((kb + 32, 128), BF16),
                pltpu.VMEM((kb, 128), F32),
                pltpu.VMEM((2, n_sky, 2, (kb + 32) // 2, 128), BF16),
                pltpu.VMEM((n_sky, hours + FOLD, 128), BF16),
                pltpu.VMEM((n_sky, hours, 256), BF16),
                pltpu.VMEM((entries, 256), BF16),
                pltpu.VMEM((n_sky, entries), F32),
                pltpu.VMEM((n_sky, ROWS + FOLD, 128), BF16),
                pltpu.VMEM((n_sky, ROWS + FOLD, 128), BF16),
                pltpu.VMEM((wins // 8, all_sens, 8 * kb), BF16),
                pltpu.VMEM((n_sky, hours, all_sens), F32),
                pltpu.VMEM((n_sky, hours, all_sens), BF16),
                pltpu.VMEM((n_sky, hours, all_sens), BF16),
                pltpu.VMEM((16, 128), BF16),
                pltpu.VMEM((2, 16, 128), BF16),
                dma((7,)), dma, dma((2,)), dma((2,)), dma, dma, dma, dma, dma, dma((n_sky,)), dma, dma, dma((2,)), dma((2,)), dma, dma,
            ],
            compiler_params=pltpu.CompilerParams(
                collective_id=0 if first else 1, has_side_effects=True, vmem_limit_bytes=56 * 2**20),
        )(*(() if first else (jnp.reshape(number, (1, 1)).astype(jnp.int32),)), *args)

    out, flag = call(True, 0)

    def in_rounds():
        rounds = -(-entries // ROWS)
        return lax.fori_loop(0, rounds, lambda i, acc: acc + call(False, i)[0], jnp.zeros_like(out))

    return lax.cond(flag[0, 0] > HUGE / 1e6, in_rounds, lambda: out)[None]


def solution(mesh):
    in_specs = (
        P(None, "sky"),
        P("sensor", "sky", None, None),
        P("sensor", None, None),
        P("sensor", "sky"),
        P("sensor", "sky", None, None),
        P("sensor", "sky", None),
        P("sensor", "sky"),
    )
    return jax.shard_map(body, mesh=mesh, in_specs=in_specs, out_specs=P("sensor", "sky", None), check_vma=False)
```

```python
import jax
import jax.numpy as jnp
from jax import lax
from jax.experimental import pallas as pl
from jax.experimental.pallas import tpu as pltpu
from jax.sharding import PartitionSpec as P

F32 = jnp.float32
BF16 = jnp.bfloat16
MESH = pl.DeviceIdType.MESH
ROWS = 48
FOLD = 16
STEP = 24
NOTE = 80
HUGE = 1e30


def up(n, m):
    return -(-n // m) * m


def iota(shape, dim):
    return lax.broadcasted_iota(jnp.int32, shape, dim)


def dot(a, b, dims=((1,), (0,))):
    return lax.dot_general(a, b, (dims, ((), ())), preferred_element_type=F32)


def fold(x, rows):
    parts = [x[g * rows : (g + 1) * rows] for g in range(x.shape[0] // rows)]
    return sum([p if g == 0 else pltpu.roll(p, g * STEP, 1) for g, p in enumerate(parts)])


def unfold(x, groups):
    return jnp.concatenate([x if g == 0 else pltpu.roll(x, 128 - g * STEP, 1) for g in range(groups)], axis=0)


def kernel(dims, first, round_ref, sky_hbm, day_hbm, bsdf_hbm, ids_hbm, view_hbm, vis_hbm, counts_hbm, out_ref, flag_ref,
           sky_ref, day, bsdf_ref, ids_ref, view_ref, vis_ref, counts_ref, wide, days, mats, own, tail, store, hours_in, skies, vpad, rank, send, got, dense, light, outs, ins, fown, fgot,
           in_sem, loc_sem, z_send, z_recv, s_send, s_recv, v_send, v_recv, p_send, p_recv, b_send, b_recv,
           f_send, f_recv, o_send, o_recv):
    n_sky, n_sen, bins, patches, wins, sens, slots, hours = dims
    nz = n_sen // 2
    kb = up(bins, 16)
    half = (kb + 32) // 2
    entries = sens * slots
    me = lax.axis_index("sky")
    mine = lax.axis_index("sensor")
    z, core = mine // 2, lax.rem(mine, 2)
    sibling = z * 2 + (1 - core)
    near, far = me, lax.rem(me + nz // 2, nz)

    def plane(shift, c):
        return lax.rem(z + shift + nz, nz) * 2 + c

    load_sky, load_day, load_bsdf, load_ids, load_view, load_vis, load_counts = [
        pltpu.make_async_copy(src, dst, in_sem.at[i])
        for i, (src, dst) in enumerate((
            (sky_hbm, sky_ref), (day_hbm, day), (bsdf_hbm, bsdf_ref), (ids_hbm, ids_ref), (view_hbm, view_ref),
            (vis_hbm, vis_ref), (counts_hbm, counts_ref)))
    ]

    def all_of(ref, sem, n):
        return pltpu.make_async_copy(ref.at[pl.ds(0, n)], ref.at[pl.ds(0, n)], sem)

    barrier = pltpu.get_barrier_semaphore()

    def greet(other_sky, other_sensor):
        pl.semaphore_signal(barrier, inc=1, device_id=(other_sky, other_sensor), device_id_type=MESH)

    def greet_sky(k, c):
        greet(lax.rem(me + k, n_sky), mine)
        return c

    if n_sky == 16:
        steps = sorted(range(1, 16), key=lambda k: -min(k // 4, 4 - k // 4) - min(k % 4, 4 - k % 4))
        others = [lax.rem(me // 4 + k // 4, 4) * 4 + lax.rem(lax.rem(me, 4) + k % 4, 4) for k in steps]
    else:
        others = [lax.rem(me + k, n_sky) for k in range(1, n_sky)]
    near_other, far_other = near != 0, far != 0

    @pl.when(near_other)
    def _():
        greet(me, plane(near, core))

    @pl.when(far_other)
    def _():
        greet(me, plane(far, core))

    if first:
        greet(me, plane(near, 1 - core))
    lax.fori_loop(1, n_sky, greet_sky, 0)
    greet(me, sibling)

    for load in (load_bsdf, load_vis, load_counts, load_view, load_sky, load_ids, load_day):
        load.start()

    own[0:kb, :] = jnp.zeros((kb, 128), BF16)
    load_bsdf.wait()
    own[0:bins, :] = bsdf_ref[:, 0:128]
    tail[...] = jnp.zeros(tail.shape, F32)
    tail[0:bins, 0 : bins - 128] = bsdf_ref[:, 128:bins].astype(F32)
    own[kb : kb + 32, :] = fold(tail[...], 32).astype(BF16)
    ins[me] = jnp.zeros(ins.shape[1:], BF16)

    load_vis.wait()
    load_counts.wait()
    vis = vis_ref[...]
    owner = vis // wins
    local = vis - owner * wins
    spread = (lax.rem(iota((slots, entries), 1), slots) == iota((slots, entries), 0)).astype(BF16)
    sensor_of = iota((sens, entries), 1) // slots == iota((sens, entries), 0)

    def flat(x):
        return jnp.sum(jnp.where(sensor_of, dot(x.astype(F32).astype(BF16), spread), 0.0), axis=0, keepdims=True)

    owner_row, local_row = flat(owner), flat(local)
    slot_row = lax.rem(iota((1, entries), 1), slots).astype(F32)
    sens_row = (iota((1, entries), 1) // slots).astype(F32)
    counts = jnp.broadcast_to(counts_ref[...].astype(F32), (16, sens)).astype(BF16)
    count_row = dot(counts, sensor_of.astype(BF16))[0:1]
    live = slot_row < count_row
    goes = jnp.logical_and(iota((n_sky, entries), 0).astype(F32) == owner_row, live)
    goes_f = goes.astype(F32)
    earlier = (iota((entries, entries), 0) < iota((entries, entries), 1)).astype(BF16)
    ranks = dot(goes_f.astype(BF16), earlier) - (0 if first else (round_ref[0, 0] * ROWS).astype(F32))
    rank[...] = jnp.where(jnp.logical_and(goes, ranks >= 0.0), ranks, -1000.0)
    most = jnp.max(jnp.sum(goes_f, axis=1, keepdims=True), axis=0, keepdims=True)
    over = jnp.where(most > ROWS, 1.0, 0.0)

    load_view.wait()
    vpad[...] = jnp.zeros(vpad.shape, BF16)
    vpad[:, 0:bins] = view_ref[...]
    note_row = iota((FOLD, entries), 0)
    notes = jnp.where(note_row == 0, local_row + 1.0, jnp.where(note_row == 1, sens_row, 0.0)).astype(BF16)
    place = (iota((128, entries), 0) - NOTE).astype(F32)
    at_flag = jnp.logical_and(iota((FOLD, 128), 0) == 2, iota((FOLD, 128), 1) >= NOTE)
    flag_note = jnp.where(at_flag, over, 0.0)

    def pack(q, c):
        pick = (place == rank[pl.ds(q, 1), :]).astype(BF16)
        rows = dot(pick[NOTE : NOTE + ROWS], vpad[...])
        send[q, 0:ROWS, :] = rows[:, 0:128].astype(BF16)
        notes_at = dot(notes, pick, ((1,), (1,)))
        send[q, ROWS : ROWS + FOLD, :] = (fold(rows[:, 128:256], FOLD) + notes_at + flag_note).astype(BF16)
        return c

    lax.fori_loop(0, n_sky, pack, 0, unroll=4 if n_sky % 4 == 0 else 1)

    pl.semaphore_wait(barrier, n_sky + (1 if first else 0) + near_other.astype(jnp.int32) + far_other.astype(jnp.int32))

    def along(i, to, c):
        return pltpu.make_async_remote_copy(
            src_ref=own.at[pl.ds(i * half, half)], dst_ref=store.at[core, me, i], send_sem=z_send.at[i],
            recv_sem=z_recv.at[i], device_id=(me, plane(-to, c)), device_id_type=MESH)

    def stay(i):
        return pltpu.make_async_copy(own.at[pl.ds(i * half, half)], store.at[core, me, i], z_recv.at[i])

    for i, to, other in ((0, near, near_other), (1, far, far_other)):

        @pl.when(other)
        def _(i=i, to=to):
            along(i, to, core).start()

        @pl.when(jnp.logical_not(other))
        def _(i=i):
            stay(i).start()

    def message(q):
        return pltpu.make_async_remote_copy(
            src_ref=send.at[q], dst_ref=got.at[me], send_sem=v_send, recv_sem=v_recv,
            device_id=(q, mine), device_id_type=MESH)

    def put(k, c):
        message(lax.rem(me + k, n_sky)).start()
        return c

    lax.fori_loop(1, n_sky, put, 0)
    keep = pltpu.make_async_copy(send.at[me], got.at[me], loc_sem)
    keep.start()

    def in_plane(q, slot):
        return pltpu.make_async_remote_copy(
            src_ref=store.at[core, slot], dst_ref=store.at[core, slot], send_sem=p_send, recv_sem=p_recv.at[slot],
            device_id=(q, mine), device_id_type=MESH)

    def across(c, slot):
        return pltpu.make_async_remote_copy(
            src_ref=store.at[c, slot], dst_ref=store.at[c, slot], send_sem=b_send, recv_sem=b_recv,
            device_id=(me, sibling), device_id_type=MESH)

    for i in range(2):
        stay(i).wait()

    for q in others:
        in_plane(q, me).start()
    across(core, me).start()

    load_sky.wait()
    tail[0:hours, :] = jnp.zeros((hours, 128), F32)
    tail[0:hours, 0 : patches - 128] = sky_ref[:, 128:patches].astype(F32)
    hours_in[me, 0:hours, :] = sky_ref[:, 0:128]
    hours_in[me, hours:, :] = fold(tail[0:hours, :], FOLD).astype(BF16)

    def put_hours(k, c):
        pltpu.make_async_remote_copy(
            src_ref=hours_in.at[me], dst_ref=hours_in.at[me], send_sem=s_send, recv_sem=s_recv,
            device_id=(lax.rem(me + k, n_sky), mine), device_id_type=MESH).start()
        return c

    lax.fori_loop(1, n_sky, put_hours, 0)

    wide[1] = jnp.zeros(wide.shape[1:], F32)
    wide[0, bins * wins :, :] = jnp.zeros((wide.shape[1] - bins * wins, 128), F32)
    load_day.wait()

    def widen(b, c):
        x = day[b].astype(F32)
        rows = pl.ds(pl.multiple_of(b * wins, 8), wins)
        wide[0, rows, :] = x[:, 0:128]
        wide[1, rows, 0 : patches - 128] = x[:, 128:patches]
        return c

    lax.fori_loop(0, bins, widen, 0, unroll=5 if bins % 5 == 0 else 1)

    def by_window(w, c):
        for i in range(2):
            days[w, :, i * 128 : i * 128 + 128] = wide[i, pl.ds(w, kb, stride=wins), :].astype(BF16)
        return c

    lax.fori_loop(0, wins, by_window, 0)

    keep.wait()

    all_of(got, v_recv, n_sky - 1).wait()
    if first:
        flags = jnp.zeros((FOLD, 128), F32)
        for q in range(n_sky):
            flags = jnp.maximum(flags, got[q, ROWS : ROWS + FOLD, :].astype(F32))
        fown[...] = jnp.broadcast_to(flags[2:3, 127:128], fown.shape).astype(BF16)

        def flag_copy(i, c):
            return pltpu.make_async_remote_copy(
                src_ref=fown, dst_ref=fgot.at[i], send_sem=f_send.at[i], recv_sem=f_recv.at[i],
                device_id=(me, plane(-near, c)), device_id_type=MESH)

        flag_stay = pltpu.make_async_copy(fown, fgot.at[0], f_recv.at[0])

        @pl.when(near_other)
        def _():
            flag_copy(0, core).start()

        @pl.when(jnp.logical_not(near_other))
        def _():
            flag_stay.start()

        flag_copy(1, 1 - core).start()

    which = iota((wins // 4 * sens, ROWS), 0).astype(F32)
    keep_tail = iota((ROWS, 128), 1) < kb - 128

    def unpack(q, c):
        folded = got[q, ROWS : ROWS + FOLD, :].astype(F32)
        note = pltpu.roll(folded, 128 - NOTE, 1)[:, 0:ROWS]
        window = note[0:1] - 1.0
        four = jnp.floor(window * 0.25)
        place_in = window - 4.0 * four
        target = four * float(sens) + note[1:2]
        ends = jnp.where(keep_tail, unfold(folded, ROWS // FOLD), 0.0)
        rows = jnp.concatenate([got[q, 0:ROWS, :].astype(F32), ends], axis=1)
        parts = []
        for m in range(4):
            pick = (which == jnp.where(place_in == float(m), target, -1.0)).astype(BF16)
            moved = rows if m == 0 else pltpu.roll(rows, m * (kb - 128), 1)
            parts.append(dot(pick, moved.astype(BF16)))
        at = pl.ds(pl.multiple_of(q * sens, sens), sens)
        for t in range(5):
            tile = parts[t][:, 0:128] if t < 4 else parts[3][:, 128:256]
            if 0 < t < 4:
                tile = tile + parts[t - 1][:, 128:256]
            tile = tile.astype(BF16).reshape(wins // 8, 2, sens, 128)
            for h in range(2):
                dense[:, at, h * 4 * kb + t * 128 : h * 4 * kb + t * 128 + 128] = tile[:, h]
        return c

    lax.fori_loop(0, n_sky, unpack, 0, unroll=2 if n_sky % 2 == 0 else 1)

    for q in others[::-1]:
        in_plane(q, q).wait_recv()
        across(core, q).start()

    all_of(hours_in, s_recv, n_sky - 1).wait()

    def unfold_hours(q, c):
        skies[q, :, 0:128] = hours_in[q, 0:hours, :]
        skies[q, :, 128:256] = unfold(hours_in[q, hours:, :].astype(F32), hours // FOLD).astype(BF16)
        return c

    lax.fori_loop(0, n_sky, unfold_hours, 0, unroll=4 if n_sky % 4 == 0 else 1)
    load_ids.wait()
    all_of(store.at[1 - core], b_recv, n_sky).wait()

    def through(w, c):
        table = ids_ref[0, w]
        away = table // 2 - z + nz
        a = store[table % 2, away % nz, 0]
        b = store[table % 2, (away + nz // 2) % nz, 1]
        ends = unfold(b[half - 32 :].astype(F32), kb // 32).astype(BF16)
        whole = jnp.concatenate([jnp.concatenate([a, b[0 : half - 32]], axis=0), ends], axis=1)
        mats[w] = dot(whole[:, 0:kb], days[w]).astype(BF16)
        return c

    lax.fori_loop(0, wins, through, 0, unroll=20 if wins % 20 == 0 else 1)

    a = jnp.zeros((sens * n_sky, 256), F32)
    for g in range(wins // 8):
        a = a + dot(dense[g], mats[g * 8 : g * 8 + 8].reshape(8 * kb, 256))

    high = a.astype(BF16)
    low = (a - high.astype(F32)).astype(BF16)
    every = skies[...].reshape(n_sky * hours, 256)
    shares = dot(every, high, ((1,), (1,))) + dot(every, low, ((1,), (1,)))
    if first:
        flag_stay.wait()
        flag_copy(1, 1 - core).wait_recv()
        seen = jnp.maximum(fgot[0], fgot[1]).astype(F32)[0:1, 0:1]
        shares = jnp.where(seen > 0.0, HUGE, shares)
    light[...] = shares.reshape(light.shape)
    outs[...] = shares.astype(BF16).reshape(outs.shape)

    for q in others:
        pltpu.make_async_remote_copy(
            src_ref=outs.at[q], dst_ref=ins.at[me], send_sem=o_send, recv_sem=o_recv,
            device_id=(q, mine), device_id_type=MESH).start()

    all_of(ins, o_recv, n_sky - 1).wait()
    total = light[me]
    for q in range(n_sky):
        total = total + ins[q].astype(F32)
    out_ref[...] = total
    flag_ref[0, 0] = jnp.max(total[0:8, 0:128])

    for i, other in enumerate((near_other, far_other)):

        @pl.when(other)
        def _(i=i):
            along(i, near, core).wait_send()

    if first:

        @pl.when(near_other)
        def _():
            flag_copy(0, core).wait_send()

        flag_copy(1, 1 - core).wait_send()

    all_of(send, v_send, n_sky - 1).wait()
    all_of(hours_in, s_send, n_sky - 1).wait()
    all_of(store.at[core], p_send, n_sky - 1).wait()
    all_of(store.at[core], b_send, n_sky).wait()
    all_of(outs, o_send, n_sky - 1).wait()


def body(sky, daylight, bsdf, bsdf_ids, view, visible, counts):
    n_sky, n_sen = lax.axis_size("sky"), lax.axis_size("sensor")
    patches, hours = sky.shape
    _, wins, bins, _ = daylight.shape
    _, sens, slots, _ = view.shape
    kb, entries = up(bins, 32), sens * slots
    dims = (n_sky, n_sen, bins, patches, wins, sens, slots, hours)
    vmem, smem = pl.BlockSpec(memory_space=pltpu.VMEM), pl.BlockSpec(memory_space=pltpu.SMEM)
    dma, all_sens = pltpu.SemaphoreType.DMA, sens * n_sky
    args = (sky.T, jnp.transpose(daylight[0], (1, 0, 2)), bsdf[0], bsdf_ids, view[0].reshape(entries, bins), visible[0], counts)

    def call(first, number):
        def run(*refs):
            if first:
                refs = (None,) + refs
            kernel(dims, first, *refs)

        return pl.pallas_call(
            run,
            out_shape=(jax.ShapeDtypeStruct((hours, all_sens), F32), jax.ShapeDtypeStruct((1, 1), F32)),
            in_specs=([] if first else [smem]) + [pl.BlockSpec(memory_space=pl.ANY)] * 7,
            out_specs=(vmem, smem),
            scratch_shapes=[
                pltpu.VMEM((hours, patches), BF16),
                pltpu.VMEM((bins, wins, patches), BF16),
                pltpu.VMEM((bins, bins), BF16),
                pltpu.SMEM((1, wins), jnp.int32),
                pltpu.VMEM((entries, bins), BF16),
                pltpu.VMEM((sens, slots), jnp.int32),
                pltpu.VMEM((1, sens), jnp.int32),
                pltpu.VMEM((2, kb * wins, 128), F32),
                pltpu.VMEM((wins, kb, 256), BF16),
                pltpu.VMEM((wins, kb, 256), BF16),
                pltpu.VMEM((kb + 32, 128), BF16),
                pltpu.VMEM((kb, 128), F32),
                pltpu.VMEM((2, n_sky, 2, (kb + 32) // 2, 128), BF16),
                pltpu.VMEM((n_sky, hours + FOLD, 128), BF16),
                pltpu.VMEM((n_sky, hours, 256), BF16),
                pltpu.VMEM((entries, 256), BF16),
                pltpu.VMEM((n_sky, entries), F32),
                pltpu.VMEM((n_sky, ROWS + FOLD, 128), BF16),
                pltpu.VMEM((n_sky, ROWS + FOLD, 128), BF16),
                pltpu.VMEM((wins // 8, all_sens, 8 * kb), BF16),
                pltpu.VMEM((n_sky, hours, all_sens), F32),
                pltpu.VMEM((n_sky, hours, all_sens), BF16),
                pltpu.VMEM((n_sky, hours, all_sens), BF16),
                pltpu.VMEM((16, 128), BF16),
                pltpu.VMEM((2, 16, 128), BF16),
                dma((7,)), dma, dma((2,)), dma((2,)), dma, dma, dma, dma, dma, dma((n_sky,)), dma, dma, dma((2,)), dma((2,)), dma, dma,
            ],
            compiler_params=pltpu.CompilerParams(
                collective_id=0 if first else 1, has_side_effects=True, vmem_limit_bytes=56 * 2**20),
        )(*(() if first else (jnp.reshape(number, (1, 1)).astype(jnp.int32),)), *args)

    out, flag = call(True, 0)

    def in_rounds():
        rounds = -(-entries // ROWS)
        return lax.fori_loop(0, rounds, lambda i, acc: acc + call(False, i)[0], jnp.zeros_like(out))

    return lax.cond(flag[0, 0] > HUGE / 1e6, in_rounds, lambda: out)[None]


def solution(mesh):
    in_specs = (
        P(None, "sky"),
        P("sensor", "sky", None, None),
        P("sensor", None, None),
        P("sensor", "sky"),
        P("sensor", "sky", None, None),
        P("sensor", "sky", None),
        P("sensor", "sky"),
    )
    return jax.shard_map(body, mesh=mesh, in_specs=in_specs, out_specs=P("sensor", "sky", None), check_vma=False)
```
